512 devices in a mesh: pin: 64 (over y, z), grp: 8 (over x, core).
Axes of the slice: x: 4, y: 8, z: 8, core: 2. Of those that a mesh axis runs over, the one named last changes fastest.
Arguments:
- slab: bfloat16 [65536, 512], P('pin'), may hold values from -6 to 6
- scales: bfloat16 [65536, 4], P('pin'), may hold values from 0.25 to 4
- owner: int32 [1081344, 1], P(('pin', 'grp')), may hold values from 0 to 63; in each aligned block of 2112 rows (0 to 2111, 2112 to 4223, ...) at most 77 rows name the same one
- local: int32 [1081344, 1], P(('pin', 'grp')), may hold values from 0 to 1023
- importance: float32 [98304, 10], P(('pin', 'grp')), may hold values from 0.05 to 1
- q_weight: bfloat16 [512, 1024], replicated, may hold values from -0.25 to 0.25
- q_bias: float32 [1024], replicated, may hold values from -3 to 3
- w_weight: bfloat16 [1536, 1024], P('pin'), may hold values from -0.15625 to 0.15625
- w_bias: float32 [1024], replicated, may hold values from -3 to 3
Outputs:
- embedded: bfloat16 [98304, 1024], P(('pin', 'grp'))
- grad_q: float32 [512, 1024], replicated
- grad_bias: float32 [1024], replicated
- loss: float32 [], replicated
The draws below stay inside these ranges and needn't reach their ends.
Inputs may be any that keep to these rules, and one draw needn't show every extreme that they name: In the 2112 rows of one device no owner is named more than 77 times, a bound that some block reaches.
All inputs are finite; a program needn't handle non-finite values.
Results may differ from the reference program's by a relative error of at most 0.011.
Values may be sent and summed in bfloat16 or wider, within the bound.
No kernel may reach another device: no remote copies, remote signals or barrier semaphores. Data moves between devices by JAX's collectives and lax.ppermute only.
A program may use at most 128 MiB of HBM per device.

```python
import math
import jax
import jax.numpy as jnp
import numpy as np
from jax import lax

F = 512
H = 1024
K = 10
BLK = 128
PAIRS = 64
NEG_DEV = 64
PIN_DEV = 1024
T_DEV = 192
REQ_DEV = 2112
CAP = 77
NEG_GRP = 512
TARGETS = 98304
REQUESTS = 1081344
PINS = 65536
N_PIN = 64
N_GRP = 8
DEVICES = 512


def plant(drawn, stream_key, smallest, top_value):
    place = [jax.random.randint(jax.random.fold_in(stream_key, axis), (), 0, length) for axis, length in enumerate(drawn.shape)]
    widest = drawn.shape.index(max(drawn.shape))
    neighbour = place[:widest] + [(place[widest] + 1) % drawn.shape[widest]] + place[widest + 1:]
    return drawn.at[tuple(place)].set(smallest).at[tuple(neighbour)].set(top_value)


def steps_of(key, dims, cuts, smallest, top_value):
    gain, own = 1.0, jax.random.fold_in(key, 6)
    for axis_at, blocks in cuts:
        steps = jnp.exp(jax.random.uniform(jax.random.fold_in(own, axis_at), (blocks,), jnp.float32, smallest / len(cuts), top_value / len(cuts)))
        gain = gain * jnp.repeat(steps, dims[axis_at] // blocks).reshape([-1 if axis == axis_at else 1 for axis in range(len(dims))])
    return gain


def deal_out(key, own, number, rows, amount, top, limit, slope):
    ranking = jax.random.permutation(key, amount)
    crowded, ordinary = load_shares(amount, rows * top, limit, slope, True), load_shares(amount, rows * top, limit, slope, False)
    places = jnp.arange(amount)

    def named(sizes, rotation):
        used = int((sizes > 0).sum())
        fixed = max(1, used // 4)
        passed = fixed + (places - fixed + rotation * (used - fixed)) % max(1, amount - fixed)
        return jnp.zeros((amount,), jnp.int32).at[ranking[jnp.where(places < fixed, places, passed)]].set(jnp.asarray(sizes, jnp.int32))

    sizes = jnp.where(number % 4 == 0, named(crowded, number // 4), named(ordinary, number - number // 4 - 1))
    mixed = jax.random.permutation(jax.random.fold_in(own, 3), amount)
    source_of, sink = mixed[0:amount // 2 * 2:2], mixed[1:amount // 2 * 2:2]
    room = jnp.minimum(sizes[source_of] - 1, limit - sizes[sink]) // 2
    room = jnp.where((source_of == ranking[0]) | (sink == ranking[0]) | (sizes[sink] == 0), 0, jnp.maximum(room, 0))
    passed = jax.random.randint(jax.random.fold_in(own, 4), (amount // 2,), 0, 1 << 20) % (room + 1)
    sizes = sizes.at[source_of].add(-passed).at[sink].add(passed)
    labels = jnp.searchsorted(jnp.cumsum(sizes), jnp.arange(rows * top), side="right").astype(jnp.int32)
    table = labels.reshape(top, rows).T
    table = table[jax.random.permutation(jax.random.fold_in(own, 1), rows)]
    rotation = jax.random.randint(jax.random.fold_in(own, 2), (rows, 1), 0, top)
    return jnp.take_along_axis(table, (jnp.arange(top)[None, :] + rotation) % top, axis=1)


def load_shares(number_of, total, limit, slope, full):
    weights = [(1 << 20) // math.isqrt(grade ** slope) + 1 for grade in range(1, number_of + 1)]
    largest = limit if full else min(limit, max(-(-total // number_of), total * weights[0] // sum(weights)))
    least = 1 if total - largest >= number_of - 1 else 0
    given, spare = [largest] + [least] * (number_of - 1), total - largest - least * (number_of - 1)
    while spare > 0:
        movable = [i for i in range(1, number_of) if given[i] < largest] or [i for i in range(1, number_of) if given[i] < limit]
        mass, remaining = sum([weights[i] for i in movable]), spare
        for i in movable:
            addition = min(limit - given[i], max(1, remaining * weights[i] // mass), spare)
            given[i] = given[i] + addition
            spare = spare - addition
    return np.array(given)


def normal_values(own_key, dims, deviation, limit, shards=(), dtype=jnp.bfloat16):
    result = jax.random.normal(own_key, dims, jnp.float32) * deviation
    if len(shards) > 0:
        result = steps_of(own_key, dims, shards, -0.22, 0.18) * result
    return jnp.clip(result, min=-limit, max=limit).astype(dtype)


def setup_inputs(seed: int = 0) -> dict:
    key_list = jax.random.split(jax.random.key(seed), 10)
    slab = normal_values(key_list[0], (PINS, F), 1.0, 6.0, ((0, 64),))
    scales = jnp.clip(jnp.exp(math.log(4.0) - 2.7725887 * jax.random.uniform(key_list[1], (PINS, F // BLK), jnp.float32) ** steps_of(key_list[1], (PINS, F // BLK), ((0, 64),), -0.2, 0.2)), 0.25, 4.0).astype(jnp.bfloat16)
    owner_keys = jax.random.split(jax.random.fold_in(key_list[2], 1), REQUESTS // REQ_DEV)
    owner_turns = jax.random.permutation(jax.random.fold_in(key_list[2], 3), REQUESTS // REQ_DEV)
    owner = jax.vmap(lambda own, number: deal_out(jax.random.fold_in(key_list[2], 2), own, number, REQ_DEV, N_PIN, 1, CAP, 2))(owner_keys, owner_turns).reshape((REQUESTS, 1))
    local = plant(jax.random.randint(key_list[3], (REQUESTS, 1), 0, PIN_DEV), jax.random.fold_in(key_list[3], 1), 0, PIN_DEV - 1).astype(jnp.int32)
    importance = jnp.clip(jnp.exp(math.log(1.0) - 2.9957323 * jax.random.uniform(key_list[4], (TARGETS, K), jnp.float32) ** steps_of(key_list[4], (TARGETS, K), ((0, 512),), -0.2, 0.2)), 0.05, 1.0)
    q_weight = normal_values(key_list[5], (F, H), F ** -0.5, 0.25)
    q_bias = normal_values(key_list[6], (H,), 0.5, 3.0, (), jnp.float32)
    w_weight = normal_values(key_list[7], (F + H, H), (F + H) ** -0.5, 0.15625, ((0, 64),))
    w_bias = normal_values(key_list[8], (H,), 0.5, 3.0, (), jnp.float32)
    return {"slab": slab, "scales": scales, "owner": owner, "local": local, "importance": importance, "q_weight": q_weight, "q_bias": q_bias, "w_weight": w_weight, "w_bias": w_bias}


margin = 0.5
score_scale = 8.0
epsilon = 1e-05

def silu_slope(value):
    gate = jax.nn.sigmoid(value)
    return gate * (1.0 + value * (1.0 - gate))

def dequantize(slab, scales, owner_ids, local_ids):
    pin_ids = owner_ids * PIN_DEV + local_ids
    raw_rows = jnp.take(slab, pin_ids, axis=0).astype(jnp.float32)
    factor = jnp.repeat(jnp.take(scales, pin_ids, axis=0).astype(jnp.float32), BLK, axis=1)
    return (raw_rows * factor).astype(jnp.bfloat16)

def forward(fetched, weights, q_weight, q_bias, w_weight, w_bias):
    grouped = fetched.reshape(T_DEV, K + 1, F)
    own_rows = grouped[:, 0]
    near_rows = grouped[:, 1:].reshape(T_DEV * K, F)
    inner = jnp.dot(near_rows, q_weight, preferred_element_type=jnp.float32) + q_bias
    shares = weights / lax.optimization_barrier(jnp.sum(weights, axis=1, keepdims=True))
    pooled = lax.optimization_barrier(jnp.sum(shares[:, :, None] * jax.nn.silu(inner).reshape(T_DEV, K, H), axis=1)).astype(jnp.bfloat16)
    joined = jnp.concatenate([own_rows, pooled], axis=1)
    outer = jnp.dot(joined, w_weight, preferred_element_type=jnp.float32) + w_bias
    active = jax.nn.silu(outer)
    scaling = lax.rsqrt(lax.optimization_barrier(jnp.mean(active * active, axis=1, keepdims=True)) + epsilon)
    return (active, scaling, outer, inner, shares, near_rows)

def reference(slab, scales, owner, local, importance, q_weight, q_bias, w_weight, w_bias):
    owner_blocks = owner.reshape(DEVICES, REQ_DEV)
    local_blocks = local.reshape(DEVICES, REQ_DEV)
    weight_blocks = importance.reshape(DEVICES, T_DEV, K)

    def embed(item):
        fetched = dequantize(slab, scales, item[0], item[1])
        active, scaling = forward(fetched, item[2], q_weight, q_bias, w_weight, w_bias)[:2]
        return (active * scaling).astype(jnp.bfloat16)
    embedded = lax.map(embed, (owner_blocks, local_blocks, weight_blocks))
    groups = embedded.reshape(N_PIN, N_GRP, T_DEV, H)

    def group_terms(members):
        queries = members[:, :PAIRS].astype(jnp.float32)
        positives = members[:, PAIRS:2 * PAIRS].astype(jnp.float32)
        negatives = members[:, 2 * PAIRS:].reshape(NEG_GRP, H).astype(jnp.float32)
        close = lax.optimization_barrier(jnp.sum(queries * positives, axis=2)) / H
        far = jnp.einsum('gph,nh->gpn', queries, negatives) / H
        margins = score_scale * (far - close[:, :, None]) + margin
        objective = jnp.sum(jax.nn.softplus(margins)) / NEG_GRP
        coef_low = (jax.nn.sigmoid(margins) * (score_scale / (NEG_GRP * H))).astype(jnp.bfloat16)
        coef = lax.optimization_barrier(coef_low).astype(jnp.float32)
        row_total = lax.optimization_barrier(jnp.sum(coef, axis=2))
        toward = jnp.einsum('gpn,nh->gph', coef, negatives) - row_total[:, :, None] * positives
        back_pos = -row_total[:, :, None] * queries
        back_neg = jnp.einsum('gpn,gph->nh', coef, queries).reshape(N_GRP, NEG_DEV, H)
        return (jnp.concatenate([toward, back_pos, back_neg], axis=1), objective)
    cotangents, objectives = lax.map(group_terms, groups)
    cotangents = cotangents.reshape(DEVICES, T_DEV, H)

    def accumulate(carry, item):
        fetched = dequantize(slab, scales, item[0], item[1])
        active, scaling, outer, inner, shares, near_rows = forward(fetched, item[2], q_weight, q_bias, w_weight, w_bias)
        d_embed = item[3]
        d_active = scaling * (d_embed - active * (lax.optimization_barrier(jnp.sum(d_embed * active, axis=1, keepdims=True)) * scaling * scaling / H))
        d_outer = (d_active * silu_slope(outer)).astype(jnp.bfloat16)
        d_joined = lax.dot_general(d_outer, w_weight, (((1,), (1,)), ((), ())), preferred_element_type=jnp.float32)
        d_pooled = d_joined[:, F:]
        spread = (shares[:, :, None] * d_pooled[:, None, :]).reshape(T_DEV * K, H)
        d_inner = (spread * silu_slope(inner)).astype(jnp.bfloat16)
        grad_q = lax.dot_general(near_rows, d_inner, (((0,), (0,)), ((), ())), preferred_element_type=jnp.float32)
        grad_bias = lax.optimization_barrier(jnp.sum(d_inner.astype(jnp.float32), axis=0))
        return ((carry[0] + grad_q, carry[1] + grad_bias), None)
    start_carry = (jnp.zeros((F, H), jnp.float32), jnp.zeros((H,), jnp.float32))
    totals, unused = lax.scan(accumulate, start_carry, (owner_blocks, local_blocks, weight_blocks, cotangents))
    loss = jnp.sum(objectives) / (PAIRS * DEVICES)
    return (embedded.reshape(TARGETS, H), totals[0], totals[1], loss)
```

```python
import jax
import jax.numpy as jnp
from jax import lax
from jax.experimental import pallas as pl
from jax.experimental.pallas import tpu as pltpu
from jax.sharding import Mesh
from jax.sharding import PartitionSpec as P

K = 10
PAIRS = 64
NEG_DEV = 64
SLOTS = 80
EXTRA = 128

margin = 0.5
score_scale = 8.0
epsilon = 1e-05

PIN = ("y", "z")
GRP = ("x", "core")
bf16 = jnp.bfloat16
f32 = jnp.float32
VMEM = 48 * 1024 * 1024


def sigmoid(value):
    return 0.5 * jnp.tanh(0.5 * value) + 0.5


def params():
    return pltpu.CompilerParams(vmem_limit_bytes=VMEM)


def row_dot(a, b):
    return lax.dot_general(a, b, (((1,), (1,)), ((), ())), preferred_element_type=f32)


def col_dot(a, b):
    return lax.dot_general(a, b, (((0,), (0,)), ((), ())), preferred_element_type=f32)


def plan_kernel(owner_ref, local_ref, wanted_ref, place_ref):
    blocks, width = owner_ref.shape
    owners = wanted_ref.shape[0]
    owner_ids = lax.broadcasted_iota(jnp.int32, (owners, width), 0)
    slot_ids = lax.broadcasted_iota(jnp.int32, (width, width), 0)
    earlier = (slot_ids < lax.broadcasted_iota(jnp.int32, (width, width), 1)).astype(f32).astype(bf16)
    count = jnp.zeros((owners, 1), f32)
    high_sum = jnp.zeros((owners, width), f32)
    low_sum = jnp.zeros((owners, width), f32)
    for block in range(blocks):
        own = owner_ref[block : block + 1, :]
        wide = (own == owner_ids).astype(f32)
        low_wide = wide.astype(bf16)
        before = jnp.dot(low_wide, earlier, preferred_element_type=f32) + count
        slot = jnp.sum(wide * before, axis=0, keepdims=True).astype(jnp.int32)
        count = count + jnp.sum(wide, axis=1, keepdims=True)
        there = (slot == slot_ids).astype(f32)
        local = local_ref[block : block + 1, :]
        high_sum = high_sum + row_dot(low_wide, (there * (local >> 5).astype(f32)).astype(bf16))
        low_sum = low_sum + row_dot(low_wide, (there * (local & 31).astype(f32)).astype(bf16))
        place_ref[block : block + 1, :] = own * SLOTS + slot
    wanted_ref[...] = (high_sum * 32.0 + low_sum).astype(jnp.int32)


def plan(owner, local, owners):
    rows = owner.shape[0]
    blocks = -(-rows // 128)
    spare = blocks * 128 - rows
    owner = jnp.pad(owner[:, 0], (0, spare), constant_values=owners).reshape(blocks, 128)
    local = jnp.pad(local[:, 0], (0, spare)).reshape(blocks, 128)
    wanted, place = pl.pallas_call(
        plan_kernel,
        out_shape=(
            jax.ShapeDtypeStruct((owners, 128), jnp.int32),
            jax.ShapeDtypeStruct((blocks, 128), jnp.int32),
        ),
        compiler_params=params(),
        name="plan",
    )(owner, local)
    return wanted[:, :SLOTS], place.reshape(-1)[:rows]


def dequantize_kernel(slab_ref, scales_ref, out_ref):
    block = slab_ref.shape[1] // scales_ref.shape[1]
    for part in range(scales_ref.shape[1]):
        lanes = slice(part * block, (part + 1) * block)
        scale = scales_ref[:, part : part + 1].astype(f32)
        out_ref[:, lanes] = (slab_ref[:, lanes].astype(f32) * scale).astype(bf16)


def shares_of(importance):
    return importance / jnp.sum(importance, axis=1, keepdims=True)


def column(values, at):
    lanes = lax.broadcasted_iota(jnp.int32, values.shape, 1)
    return jnp.sum(jnp.where(lanes == at, values, 0.0), axis=1, keepdims=True)


def forward_kernel(
    own_ref,
    near_ref,
    importance_ref,
    q_weight_ref,
    q_bias_ref,
    w_ref,
    w_bias_ref,
    slope_ref,
    embedded_ref,
    active_ref,
    outer_slope_ref,
    payload_ref,
    pooled,
):
    step = pl.program_id(0)
    share = column(shares_of(importance_ref[...]), step)
    inner = jnp.dot(near_ref[...], q_weight_ref[...], preferred_element_type=f32) + q_bias_ref[...]
    gate = sigmoid(inner)
    smooth = inner * gate
    slope_ref[...] = (gate + smooth * (1.0 - gate)).astype(bf16)
    term = share * smooth

    @pl.when(step == 0)
    def _():
        pooled[...] = term

    @pl.when(step > 0)
    def _():
        pooled[...] += term

    @pl.when(step == pl.num_programs(0) - 1)
    def _():
        width = own_ref.shape[1]
        hidden = active_ref.shape[1]
        outer = (
            jnp.dot(own_ref[...], w_ref[:width, :], preferred_element_type=f32)
            + jnp.dot(pooled[...].astype(bf16), w_ref[width:, :], preferred_element_type=f32)
            + w_bias_ref[...]
        )
        gate = sigmoid(outer)
        active = outer * gate
        active_ref[...] = active
        outer_slope_ref[...] = gate + active * (1.0 - gate)
        scaling = lax.rsqrt(jnp.mean(active * active, axis=1, keepdims=True) + epsilon)
        embedded = (active * scaling).astype(bf16)
        embedded_ref[...] = embedded
        queries = embedded[:PAIRS].astype(f32)
        close = jnp.sum(queries * embedded[PAIRS : 2 * PAIRS].astype(f32), axis=1, keepdims=True)
        close = close / hidden
        first = close.astype(bf16).astype(f32)
        second = (close - first).astype(bf16).astype(f32)
        third = close - first - second
        lanes = lax.broadcasted_iota(jnp.int32, (PAIRS, EXTRA), 1)
        pieces = jnp.where(
            lanes == 0, first, jnp.where(lanes == 1, second, jnp.where(lanes == 2, third, 0.0))
        )
        payload_ref[:PAIRS, :hidden] = embedded[:PAIRS]
        payload_ref[PAIRS:, :hidden] = embedded[2 * PAIRS :]
        payload_ref[:PAIRS, hidden:] = pieces.astype(bf16)
        payload_ref[PAIRS:, hidden:] = jnp.zeros((NEG_DEV, EXTRA), bf16)


def whole(shape):
    return pl.BlockSpec(shape, lambda step: (0,) * len(shape))


def forward(fetched, importance, q_weight, q_bias, w_full, w_bias):
    targets = importance.shape[0]
    width, hidden = q_weight.shape
    sent = PAIRS + NEG_DEV
    return pl.pallas_call(
        forward_kernel,
        grid=(K,),
        in_specs=[
            pl.BlockSpec((targets, width), lambda step: (0, 0)),
            pl.BlockSpec((targets, width), lambda step: (step + 1, 0)),
            whole(importance.shape),
            whole(q_weight.shape),
            whole((1, hidden)),
            whole(w_full.shape),
            whole((1, hidden)),
        ],
        out_specs=[
            pl.BlockSpec((targets, hidden), lambda step: (step, 0)),
            whole((targets, hidden)),
            whole((targets, hidden)),
            whole((targets, hidden)),
            whole((sent, hidden + EXTRA)),
        ],
        out_shape=(
            jax.ShapeDtypeStruct((targets * K, hidden), bf16),
            jax.ShapeDtypeStruct((targets, hidden), bf16),
            jax.ShapeDtypeStruct((targets, hidden), f32),
            jax.ShapeDtypeStruct((targets, hidden), f32),
            jax.ShapeDtypeStruct((sent, hidden + EXTRA), bf16),
        ),
        scratch_shapes=[pltpu.VMEM((targets, hidden), f32)],
        compiler_params=params(),
        name="forward",
    )(fetched, fetched, importance, q_weight, q_bias[None, :], w_full, w_bias[None, :])


def backward_kernel(
    fetched_ref,
    importance_ref,
    w_ref,
    slope_ref,
    embedded_ref,
    active_ref,
    outer_slope_ref,
    group_ref,
    grad_ref,
    d_pooled,
    d_inner,
    bias_sum,
    objective_sum,
):
    step = pl.program_id(0)
    targets, hidden = active_ref.shape
    members = group_ref.shape[0]
    negatives_count = members * NEG_DEV

    @pl.when(step == 0)
    def _():
        embedded = embedded_ref[...]
        queries = embedded[:PAIRS]
        positives = embedded[PAIRS : 2 * PAIRS].astype(f32)
        negatives = embedded[2 * PAIRS :]
        group_queries = group_ref[:, :PAIRS, :hidden].reshape(members * PAIRS, hidden)
        group_negatives = group_ref[:, PAIRS:, :hidden].reshape(negatives_count, hidden)
        pieces = group_ref[:, :PAIRS, hidden:].reshape(members * PAIRS, EXTRA).astype(f32)
        group_close = jnp.sum(pieces, axis=1, keepdims=True)
        coef_factor = score_scale / (negatives_count * hidden)
        wide_queries = queries.astype(f32)
        close = jnp.sum(wide_queries * positives, axis=1, keepdims=True) / hidden
        far = row_dot(queries, group_negatives) / hidden
        margins = score_scale * (far - close) + margin
        coef = (sigmoid(margins) * coef_factor).astype(bf16)
        toward = jnp.dot(coef, group_negatives, preferred_element_type=f32)
        row_total = jnp.sum(coef.astype(f32), axis=1, keepdims=True)
        softplus = jnp.maximum(margins, 0.0) + jnp.log1p(jnp.exp(-jnp.abs(margins)))
        objective = jnp.sum(jnp.sum(softplus, axis=1, keepdims=True), axis=0, keepdims=True)
        objective_sum[...] = jnp.broadcast_to(objective / negatives_count, objective_sum.shape)
        group_far = row_dot(group_queries, negatives) / hidden
        group_margins = score_scale * (group_far - group_close) + margin
        group_coef = (sigmoid(group_margins) * coef_factor).astype(bf16)
        d_embed = jnp.concatenate(
            [
                toward - row_total * positives,
                -row_total * wide_queries,
                col_dot(group_coef, group_queries),
            ],
            axis=0,
        )
        active = active_ref[...]
        scaling = lax.rsqrt(jnp.mean(active * active, axis=1, keepdims=True) + epsilon)
        along = jnp.sum(d_embed * active, axis=1, keepdims=True)
        d_active = scaling * (d_embed - active * (along * scaling * scaling / hidden))
        d_outer = (d_active * outer_slope_ref[...]).astype(bf16)
        d_pooled[...] = row_dot(d_outer, w_ref[...])
        bias_sum[...] = jnp.zeros_like(bias_sum)

    share = column(shares_of(importance_ref[...]), step)
    d_near = (share * d_pooled[...] * slope_ref[...].astype(f32)).astype(bf16)
    d_inner[pl.ds(pl.multiple_of(step * targets, targets), targets), :] = d_near
    bias_sum[...] += jnp.sum(d_near.astype(f32), axis=0, keepdims=True)

    @pl.when(step == pl.num_programs(0) - 1)
    def _():
        near = fetched_ref[targets:, :]
        for part in range(4):
            lanes = slice(part * hidden // 4, (part + 1) * hidden // 4)
            grad_ref[:, lanes] = col_dot(near, d_inner[:, lanes]).astype(bf16)
        grad_ref[:, hidden:] = jnp.zeros((grad_ref.shape[0], EXTRA), bf16)
        rows = lax.broadcasted_iota(jnp.int32, (16, EXTRA), 0)
        small = jnp.zeros((16, EXTRA), f32)
        for part in range(hidden // EXTRA):
            piece = bias_sum[:, part * EXTRA : (part + 1) * EXTRA]
            small = jnp.where(rows == part, piece, small)
        objective = objective_sum[...]
        first = objective.astype(bf16).astype(f32)
        small = jnp.where(rows == hidden // EXTRA, first, small)
        small = jnp.where(rows == hidden // EXTRA + 1, objective - first, small)
        grad_ref[:16, hidden:] = small.astype(bf16)


def backward(fetched, importance, w_full, slope, embedded, active, outer_slope, group):
    targets, hidden = active.shape
    width = fetched.shape[1]
    return pl.pallas_call(
        backward_kernel,
        grid=(K,),
        in_specs=[
            whole(fetched.shape),
            whole(importance.shape),
            whole((hidden, hidden)),
            pl.BlockSpec((targets, hidden), lambda step: (step, 0)),
            whole(embedded.shape),
            whole(active.shape),
            whole(outer_slope.shape),
            whole(group.shape),
        ],
        out_specs=whole((width, hidden + EXTRA)),
        out_shape=jax.ShapeDtypeStruct((width, hidden + EXTRA), bf16),
        scratch_shapes=[
            pltpu.VMEM((targets, hidden), f32),
            pltpu.VMEM((targets * K, hidden), bf16),
            pltpu.VMEM((1, hidden), f32),
            pltpu.VMEM((1, EXTRA), f32),
        ],
        compiler_params=params(),
        name="backward",
    )(fetched, importance, w_full[width:], slope, embedded, active, outer_slope, group)


def exchange(values, axes):
    return lax.all_to_all(values, axes, split_axis=0, concat_axis=0, tiled=True)


def spread(values, axes):
    count = lax.axis_size(axes)
    return exchange(jnp.broadcast_to(values[None], (count,) + values.shape), axes)


def both_cores(values):
    other = lax.ppermute(values, "core", [(0, 1), (1, 0)])
    first = lax.axis_index("core") == 0
    return jnp.stack([jnp.where(first, values, other), jnp.where(first, other, values)])


def total(values, axes):
    count = lax.axis_size(axes)
    share = values.shape[0] // count
    parts = exchange(values.reshape((count, share) + values.shape[1:]), axes)
    return jnp.sum(parts.astype(f32), axis=0)


def body(slab, scales, owner, local, importance, q_weight, q_bias, w_weight, w_bias):
    pin_count = lax.axis_size(PIN)
    targets = importance.shape[0]
    width, hidden = q_weight.shape
    w_full = lax.all_gather(w_weight, PIN, axis=0, tiled=True)
    wanted, place = plan(owner, local, pin_count)
    ready = pl.pallas_call(
        dequantize_kernel,
        out_shape=jax.ShapeDtypeStruct(slab.shape, bf16),
        compiler_params=params(),
        name="dequantize",
    )(slab, scales)
    asked = exchange(wanted, PIN)
    picked = jnp.take(ready, asked.reshape(-1), axis=0, mode="clip")
    got = exchange(picked.reshape(pin_count, SLOTS, width), PIN).reshape(-1, width)
    by_neighbour = place.reshape(targets, K + 1).T.reshape(-1)
    fetched = jnp.take(got, by_neighbour, axis=0, mode="clip")
    slope, embedded, active, outer_slope, payload = forward(
        fetched, importance, q_weight, q_bias, w_full, w_bias
    )
    group = both_cores(spread(payload, "x"))
    group = group.reshape((-1,) + payload.shape)
    grads = backward(fetched, importance, w_full, slope, embedded, active, outer_slope, group)
    grads = total(grads, "core").astype(bf16)
    grads = total(grads, "x").astype(bf16)
    grads = total(grads, PIN)
    loss_row = hidden // EXTRA
    split = grads.astype(bf16)
    grads = spread(split, PIN).reshape(-1, hidden + EXTRA)
    grads = spread(grads, "x").reshape(-1, hidden + EXTRA)
    grads = both_cores(grads).reshape(-1, hidden + EXTRA)
    grad_q = grads[:, :hidden].astype(f32)
    grad_bias = grads[:loss_row, hidden:].astype(f32).reshape(-1)
    objective = jnp.sum(grads[loss_row : loss_row + 2, hidden].astype(f32))
    devices = pin_count * lax.axis_size(GRP)
    loss = objective / (PAIRS * devices)
    return (embedded, grad_q, grad_bias, loss)


def solution(mesh):
    devices = mesh.devices.reshape(8, 8, 4, 2)
    fine = Mesh(devices, PIN + GRP)
    in_specs = (
        P(PIN, None),
        P(PIN, None),
        P(PIN + GRP, None),
        P(PIN + GRP, None),
        P(PIN + GRP, None),
        P(),
        P(),
        P(PIN, None),
        P(),
    )
    out_specs = (P(PIN + GRP, None), P(), P(), P())
    return jax.shard_map(body, mesh=fine, in_specs=in_specs, out_specs=out_specs, check_vma=False)
```

```python
import jax
import jax.numpy as jnp
from jax import lax
from jax.experimental import pallas as pl
from jax.experimental.pallas import tpu as pltpu
from jax.sharding import Mesh
from jax.sharding import PartitionSpec as P

K = 10
PAIRS = 64
NEG_DEV = 64
SLOTS = 48
ALL_SLOTS = 80
PIECE = 16
DIGIT = 32
EXTRA = 128

margin = 0.5
score_scale = 8.0
epsilon = 1e-05

PIN = ("y", "z")
GRP = ("x", "core")
bf16 = jnp.bfloat16
f32 = jnp.float32
VMEM = 48 * 1024 * 1024


def sigmoid(value):
    return 0.5 * jnp.tanh(0.5 * value) + 0.5


def params():
    return pltpu.CompilerParams(vmem_limit_bytes=VMEM)


def row_dot(a, b):
    return lax.dot_general(a, b, (((1,), (1,)), ((), ())), preferred_element_type=f32)


def col_dot(a, b):
    return lax.dot_general(a, b, (((0,), (0,)), ((), ())), preferred_element_type=f32)


def before(parts):
    width = parts[0].shape[1]
    earlier = lax.broadcasted_iota(jnp.int32, (width, width), 0) < lax.broadcasted_iota(
        jnp.int32, (width, width), 1
    )
    inside = jnp.dot(
        jnp.concatenate([part.astype(bf16) for part in parts], axis=0),
        earlier.astype(f32).astype(bf16),
        preferred_element_type=f32,
    )
    high = parts[0].shape[0]
    sums, count = [], jnp.zeros((high, 1), f32)
    for block, part in enumerate(parts):
        sums.append(inside[block * high : (block + 1) * high] + count)
        count = count + jnp.sum(part, axis=1, keepdims=True)
    return sums, count


def pick(wide, values):
    return jnp.sum(wide * values, axis=0, keepdims=True)


def plan_kernel(owner_ref, local_ref, high_ref, low_ref, target_ref, slot_ref):
    blocks, width = owner_ref.shape
    owners = high_ref.shape[0]
    ids = lax.broadcasted_iota(jnp.int32, (owners, width), 0)
    own = [owner_ref[block : block + 1, :] for block in range(blocks)]
    local = [local_ref[block : block + 1, :] for block in range(blocks)]
    first = [(one == ids).astype(f32) for one in own]
    second = [((one // PIECE) == ids).astype(f32) for one in local]
    rank, load = before(first)
    excess = jnp.maximum(load - SLOTS, 0.0)
    spare = jnp.maximum(SLOTS - load, 0.0)
    own_excess = [pick(wide, excess) for wide in first]
    other_spare = [pick(wide, spare) for wide in second]
    movable = [
        jnp.where((over > 0.0) & (room > 0.0), 1.0, 0.0)
        for over, room in zip(own_excess, other_spare)
    ]
    queue, _ = before([wide * free for wide, free in zip(second, movable)])
    queue = [pick(wide, sums) for wide, sums in zip(second, queue)]
    kept = [
        jnp.where((free > 0.0) & (place < room), 1.0, 0.0)
        for free, place, room in zip(movable, queue, other_spare)
    ]
    gone, _ = before([wide * free for wide, free in zip(first, kept)])
    slot_ids = lax.broadcasted_iota(jnp.int32, (width, width), 0)
    high_sum = jnp.zeros((owners, width), f32)
    low_sum = jnp.zeros((owners, width), f32)
    widest = jnp.zeros((1, width), jnp.int32)
    for block in range(blocks):
        gone_before = pick(first[block], gone[block])
        moved = (kept[block] > 0.0) & (gone_before < own_excess[block])
        stays = pick(first[block], rank[block]) - jnp.minimum(gone_before, own_excess[block])
        goes = pick(second[block], load) + queue[block]
        slot = jnp.where(moved, goes, stays).astype(jnp.int32)
        row = jnp.where(
            moved,
            owners * PIECE + own[block] * PIECE + local[block] % PIECE,
            local[block],
        )
        weight = jnp.where(moved, 1.0, 0.0)
        wide = (first[block] * (1.0 - weight) + second[block] * weight).astype(bf16)
        there = (slot == slot_ids).astype(f32)
        high_sum = high_sum + row_dot(wide, (there * (row // DIGIT).astype(f32)).astype(bf16))
        low_sum = low_sum + row_dot(wide, (there * (row % DIGIT).astype(f32)).astype(bf16))
        widest = jnp.maximum(widest, slot)
        target_ref[block : block + 1, :] = jnp.where(moved, local[block] // PIECE, own[block])
        slot_ref[block : block + 1, :] = slot
    over = (jnp.max(widest, axis=1, keepdims=True) >= SLOTS).astype(f32)
    last = lax.broadcasted_iota(jnp.int32, (owners, width), 1) == width - 1
    high_ref[...] = jnp.where(last, over, high_sum).astype(bf16)
    low_ref[...] = low_sum.astype(bf16)


def plan(owner, local, owners):
    rows = owner.shape[0]
    blocks = -(-rows // 128)
    spare = blocks * 128 - rows
    owner = jnp.pad(owner[:, 0], (0, spare), constant_values=owners).reshape(blocks, 128)
    local = jnp.pad(local[:, 0], (0, spare)).reshape(blocks, 128)
    high, low, target, slot = pl.pallas_call(
        plan_kernel,
        out_shape=(
            jax.ShapeDtypeStruct((owners, 128), bf16),
            jax.ShapeDtypeStruct((owners, 128), bf16),
            jax.ShapeDtypeStruct((blocks, 128), jnp.int32),
            jax.ShapeDtypeStruct((blocks, 128), jnp.int32),
        ),
        compiler_params=params(),
        name="plan",
    )(owner, local)
    return high, low, target.reshape(-1)[:rows], slot.reshape(-1)[:rows]


def dequantize_kernel(slab_ref, scales_ref, out_ref):
    block = slab_ref.shape[1] // scales_ref.shape[1]
    for part in range(scales_ref.shape[1]):
        lanes = slice(part * block, (part + 1) * block)
        scale = scales_ref[:, part : part + 1].astype(f32)
        out_ref[:, lanes] = (slab_ref[:, lanes].astype(f32) * scale).astype(bf16)


def shares_of(importance):
    return importance / jnp.sum(importance, axis=1, keepdims=True)


def column(values, at):
    lanes = lax.broadcasted_iota(jnp.int32, values.shape, 1)
    return jnp.sum(jnp.where(lanes == at, values, 0.0), axis=1, keepdims=True)


def columns(w_ref, part, start, end):
    return jnp.concatenate(
        [w_ref[2 * part, start:end, :], w_ref[2 * part + 1, start:end, :]], axis=1
    )


def forward_kernel(
    own_ref,
    near_ref,
    importance_ref,
    q_weight_ref,
    q_bias_ref,
    w_ref,
    w_bias_ref,
    slope_ref,
    embedded_ref,
    active_ref,
    outer_slope_ref,
    payload_ref,
    pooled,
):
    step = pl.program_id(0)
    share = column(shares_of(importance_ref[...]), step)
    inner = jnp.dot(near_ref[...], q_weight_ref[...], preferred_element_type=f32) + q_bias_ref[...]
    gate = sigmoid(inner)
    smooth = inner * gate
    slope_ref[...] = (gate + smooth * (1.0 - gate)).astype(bf16)
    term = share * smooth

    @pl.when(step == 0)
    def _():
        pooled[...] = term

    @pl.when(step > 0)
    def _():
        pooled[...] += term

    @pl.when(step == pl.num_programs(0) - 1)
    def _():
        width = own_ref.shape[1]
        hidden = active_ref.shape[1]
        joined = jnp.concatenate([own_ref[...], pooled[...].astype(bf16)], axis=1)
        outer = jnp.concatenate(
            [
                jnp.dot(joined, columns(w_ref, part, 0, width + hidden), preferred_element_type=f32)
                for part in range(w_ref.shape[0] // 2)
            ],
            axis=1,
        )
        outer = outer + w_bias_ref[...]
        gate = sigmoid(outer)
        active = outer * gate
        active_ref[...] = active
        outer_slope_ref[...] = gate + active * (1.0 - gate)
        scaling = lax.rsqrt(jnp.mean(active * active, axis=1, keepdims=True) + epsilon)
        embedded = (active * scaling).astype(bf16)
        embedded_ref[...] = embedded
        queries = embedded[:PAIRS].astype(f32)
        close = jnp.sum(queries * embedded[PAIRS : 2 * PAIRS].astype(f32), axis=1, keepdims=True)
        close = close / hidden
        first = close.astype(bf16).astype(f32)
        second = (close - first).astype(bf16).astype(f32)
        third = close - first - second
        lanes = lax.broadcasted_iota(jnp.int32, (PAIRS, EXTRA), 1)
        pieces = jnp.where(
            lanes == 0, first, jnp.where(lanes == 1, second, jnp.where(lanes == 2, third, 0.0))
        )
        payload_ref[:PAIRS, :hidden] = embedded[:PAIRS]
        payload_ref[PAIRS:, :hidden] = embedded[2 * PAIRS :]
        payload_ref[:PAIRS, hidden:] = pieces.astype(bf16)
        payload_ref[PAIRS:, hidden:] = jnp.zeros((NEG_DEV, EXTRA), bf16)


def whole(shape):
    return pl.BlockSpec(shape, lambda step: (0,) * len(shape))


def forward(fetched, importance, q_weight, q_bias, w_full, w_bias):
    targets = importance.shape[0]
    width, hidden = q_weight.shape
    sent = PAIRS + NEG_DEV
    return pl.pallas_call(
        forward_kernel,
        grid=(K,),
        in_specs=[
            pl.BlockSpec((targets, width), lambda step: (0, 0)),
            pl.BlockSpec((targets, width), lambda step: (step + 1, 0)),
            whole(importance.shape),
            whole(q_weight.shape),
            whole((1, hidden)),
            whole(w_full.shape),
            whole((1, hidden)),
        ],
        out_specs=[
            pl.BlockSpec((targets, hidden), lambda step: (step, 0)),
            whole((targets, hidden)),
            whole((targets, hidden)),
            whole((targets, hidden)),
            whole((sent, hidden + EXTRA)),
        ],
        out_shape=(
            jax.ShapeDtypeStruct((targets * K, hidden), bf16),
            jax.ShapeDtypeStruct((targets, hidden), bf16),
            jax.ShapeDtypeStruct((targets, hidden), f32),
            jax.ShapeDtypeStruct((targets, hidden), f32),
            jax.ShapeDtypeStruct((sent, hidden + EXTRA), bf16),
        ),
        scratch_shapes=[pltpu.VMEM((targets, hidden), f32)],
        compiler_params=params(),
        name="forward",
    )(fetched, fetched, importance, q_weight, q_bias[None, :], w_full, w_bias[None, :])


def backward_kernel(
    fetched_ref,
    importance_ref,
    w_ref,
    slope_ref,
    embedded_ref,
    active_ref,
    outer_slope_ref,
    group_ref,
    grad_ref,
    d_pooled,
    d_inner,
    bias_sum,
    objective_sum,
):
    step = pl.program_id(0)
    targets, hidden = active_ref.shape
    members = group_ref.shape[0]
    negatives_count = members * NEG_DEV

    @pl.when(step == 0)
    def _():
        embedded = embedded_ref[...]
        queries = embedded[:PAIRS]
        positives = embedded[PAIRS : 2 * PAIRS].astype(f32)
        negatives = embedded[2 * PAIRS :]
        group_queries = group_ref[:, :PAIRS, :hidden].reshape(members * PAIRS, hidden)
        group_negatives = group_ref[:, PAIRS:, :hidden].reshape(negatives_count, hidden)
        pieces = group_ref[:, :PAIRS, hidden:].reshape(members * PAIRS, EXTRA).astype(f32)
        group_close = jnp.sum(pieces, axis=1, keepdims=True)
        coef_factor = score_scale / (negatives_count * hidden)
        wide_queries = queries.astype(f32)
        close = jnp.sum(wide_queries * positives, axis=1, keepdims=True) / hidden
        far = row_dot(queries, group_negatives) / hidden
        margins = score_scale * (far - close) + margin
        coef = (sigmoid(margins) * coef_factor).astype(bf16)
        toward = jnp.dot(coef, group_negatives, preferred_element_type=f32)
        row_total = jnp.sum(coef.astype(f32), axis=1, keepdims=True)
        softplus = jnp.maximum(margins, 0.0) + jnp.log1p(jnp.exp(-jnp.abs(margins)))
        objective = jnp.sum(jnp.sum(softplus, axis=1, keepdims=True), axis=0, keepdims=True)
        objective_sum[...] = jnp.broadcast_to(objective / negatives_count, objective_sum.shape)
        group_far = row_dot(group_queries, negatives) / hidden
        group_margins = score_scale * (group_far - group_close) + margin
        group_coef = (sigmoid(group_margins) * coef_factor).astype(bf16)
        d_embed = jnp.concatenate(
            [
                toward - row_total * positives,
                -row_total * wide_queries,
                col_dot(group_coef, group_queries),
            ],
            axis=0,
        )
        active = active_ref[...]
        scaling = lax.rsqrt(jnp.mean(active * active, axis=1, keepdims=True) + epsilon)
        along = jnp.sum(d_embed * active, axis=1, keepdims=True)
        d_active = scaling * (d_embed - active * (along * scaling * scaling / hidden))
        d_outer = (d_active * outer_slope_ref[...]).astype(bf16)
        width = fetched_ref.shape[1]
        pair = 2 * w_ref.shape[2]
        sums = jnp.zeros((targets, hidden), f32)
        for part in range(w_ref.shape[0] // 2):
            lanes = slice(part * pair, (part + 1) * pair)
            sums = sums + row_dot(d_outer[:, lanes], columns(w_ref, part, width, width + hidden))
        d_pooled[...] = sums
        bias_sum[...] = jnp.zeros_like(bias_sum)

    share = column(shares_of(importance_ref[...]), step)
    d_near = (share * d_pooled[...] * slope_ref[...].astype(f32)).astype(bf16)
    d_inner[pl.ds(pl.multiple_of(step * targets, targets), targets), :] = d_near
    bias_sum[...] += jnp.sum(d_near.astype(f32), axis=0, keepdims=True)

    @pl.when(step == pl.num_programs(0) - 1)
    def _():
        near = fetched_ref[targets:, :]
        for part in range(4):
            lanes = slice(part * hidden // 4, (part + 1) * hidden // 4)
            grad_ref[:, lanes] = col_dot(near, d_inner[:, lanes]).astype(bf16)
        grad_ref[:, hidden:] = jnp.zeros((grad_ref.shape[0], EXTRA), bf16)
        rows = lax.broadcasted_iota(jnp.int32, (16, EXTRA), 0)
        small = jnp.zeros((16, EXTRA), f32)
        for part in range(hidden // EXTRA):
            piece = bias_sum[:, part * EXTRA : (part + 1) * EXTRA]
            small = jnp.where(rows == part, piece, small)
        objective = objective_sum[...]
        first = objective.astype(bf16).astype(f32)
        small = jnp.where(rows == hidden // EXTRA, first, small)
        small = jnp.where(rows == hidden // EXTRA + 1, objective - first, small)
        grad_ref[:16, hidden:] = small.astype(bf16)


def backward(fetched, importance, w_full, slope, embedded, active, outer_slope, group):
    targets, hidden = active.shape
    width = fetched.shape[1]
    return pl.pallas_call(
        backward_kernel,
        grid=(K,),
        in_specs=[
            whole(fetched.shape),
            whole(importance.shape),
            whole(w_full.shape),
            pl.BlockSpec((targets, hidden), lambda step: (step, 0)),
            whole(embedded.shape),
            whole(active.shape),
            whole(outer_slope.shape),
            whole(group.shape),
        ],
        out_specs=whole((width, hidden + EXTRA)),
        out_shape=jax.ShapeDtypeStruct((width, hidden + EXTRA), bf16),
        scratch_shapes=[
            pltpu.VMEM((targets, hidden), f32),
            pltpu.VMEM((targets * K, hidden), bf16),
            pltpu.VMEM((1, hidden), f32),
            pltpu.VMEM((1, EXTRA), f32),
        ],
        compiler_params=params(),
        name="backward",
    )(fetched, importance, w_full, slope, embedded, active, outer_slope, group)


def exchange(values, axes):
    return lax.all_to_all(values, axes, split_axis=0, concat_axis=0, tiled=True)


def spread(values, axes):
    count = lax.axis_size(axes)
    return exchange(jnp.broadcast_to(values[None], (count,) + values.shape), axes)


def total(values, axes):
    count = lax.axis_size(axes)
    share = values.shape[0] // count
    parts = exchange(values.reshape((count, share) + values.shape[1:]), axes)
    return jnp.sum(parts.astype(f32), axis=0)


def body(slab, scales, owner, local, importance, q_weight, q_bias, w_weight, w_bias):
    pin_count = lax.axis_size(PIN)
    targets = importance.shape[0]
    width, hidden = q_weight.shape
    high, low, target, slot = plan(owner, local, pin_count)
    ready = pl.pallas_call(
        dequantize_kernel,
        out_shape=jax.ShapeDtypeStruct(slab.shape, bf16),
        compiler_params=params(),
        name="dequantize",
    )(slab, scales)
    members = lax.axis_size(GRP)
    lanes = hidden // members
    rows = w_weight.shape[0]
    mine = lax.dynamic_slice_in_dim(w_weight, lax.axis_index(GRP) * lanes, lanes, 1)
    mine = mine.reshape(rows // 8, 8, lanes).transpose(1, 0, 2).reshape(8, -1)
    ids = jnp.concatenate([high[:, None], low[:, None]], axis=1)
    tail = jnp.concatenate(
        [
            jnp.broadcast_to(mine[None], (pin_count,) + mine.shape),
            jnp.pad(ids, ((0, 0), (0, 6), (0, 0))),
        ],
        axis=2,
    )
    sent = jnp.concatenate([ready.reshape(pin_count, PIECE, width), tail], axis=1)
    sent = exchange(sent, PIN)
    table = jnp.concatenate([ready, sent[:, :PIECE].reshape(pin_count * PIECE, width)], axis=0)
    ids = sent[:, PIECE : PIECE + 2, mine.shape[1] :].astype(jnp.int32)
    asked = ids[:, 0, :ALL_SLOTS] * DIGIT + ids[:, 1, :ALL_SLOTS]
    picked = jnp.take(table, asked[:, :SLOTS].reshape(-1), axis=0, mode="clip")
    got = exchange(picked.reshape(pin_count, SLOTS, width), PIN).reshape(-1, width)
    w_part = sent[:, PIECE:, : mine.shape[1]].reshape(pin_count, 8, rows // 8, lanes)
    w_part = w_part.transpose(0, 2, 1, 3).reshape(pin_count * rows, lanes)
    over = jnp.max(sent[:, PIECE, -1])
    w_part = jnp.concatenate([w_part, jnp.broadcast_to(over, (16, lanes))], axis=0)
    w_full = lax.all_gather(w_part, GRP, axis=0, tiled=False)
    over = jnp.max(w_full[:, -16:, :].astype(f32)) > 0.5

    def ordered(values):
        return values.reshape(targets, K + 1).T.reshape(-1)

    target, slot = ordered(target), ordered(slot)
    late = slot >= SLOTS
    fetched = jnp.take(got, jnp.where(late, 0, target * SLOTS + slot), axis=0, mode="clip")

    def second_exchange(fetched):
        more = ALL_SLOTS - SLOTS
        picked = jnp.take(table, asked[:, SLOTS:].reshape(-1), axis=0, mode="clip")
        got = exchange(picked.reshape(pin_count, more, width), PIN).reshape(-1, width)
        place = jnp.where(late, target * more + slot - SLOTS, 0)
        return jnp.where(late[:, None], jnp.take(got, place, axis=0, mode="clip"), fetched)

    fetched = lax.cond(over, second_exchange, lambda fetched: fetched, fetched)
    slope, embedded, active, outer_slope, payload = forward(
        fetched, importance, q_weight, q_bias, w_full, w_bias
    )
    group = spread(spread(payload, "x"), "core")
    group = group.reshape((-1,) + payload.shape)
    grads = backward(fetched, importance, w_full, slope, embedded, active, outer_slope, group)
    grads = total(grads, "core").astype(bf16)
    grads = total(grads, "x").astype(bf16)
    grads = total(grads, PIN)
    loss_row = hidden // EXTRA
    split = grads.astype(bf16)
    grads = spread(split, PIN).reshape(-1, hidden + EXTRA)
    grads = spread(grads, "x").reshape(-1, hidden + EXTRA)
    grads = spread(grads, "core").reshape(-1, hidden + EXTRA)
    grad_q = grads[:, :hidden].astype(f32)
    grad_bias = grads[:loss_row, hidden:].astype(f32).reshape(-1)
    objective = jnp.sum(grads[loss_row : loss_row + 2, hidden].astype(f32))
    devices = pin_count * lax.axis_size(GRP)
    loss = objective / (PAIRS * devices)
    return (embedded, grad_q, grad_bias, loss)


def solution(mesh):
    devices = mesh.devices.reshape(8, 8, 4, 2)
    fine = Mesh(devices, PIN + GRP)
    in_specs = (
        P(PIN, None),
        P(PIN, None),
        P(PIN + GRP, None),
        P(PIN + GRP, None),
        P(PIN + GRP, None),
        P(),
        P(),
        P(PIN, None),
        P(),
    )
    out_specs = (P(PIN + GRP, None), P(), P(), P())
    return jax.shard_map(body, mesh=fine, in_specs=in_specs, out_specs=out_specs, check_vma=False)
```

```python
import jax
import jax.numpy as jnp
from jax import lax
from jax.experimental import pallas as pl
from jax.experimental.pallas import tpu as pltpu
from jax.sharding import Mesh
from jax.sharding import PartitionSpec as P

K = 10
PAIRS = 64
NEG_DEV = 64
SLOTS = 40
ALL_SLOTS = 80
PIECE = 16
COPIED = 12
TARGETS = (44, 36, 40, 40)
DIGIT = 32
EXTRA = 128

margin = 0.5
score_scale = 8.0
epsilon = 1e-05

PIN = ("y", "z")
GRP = ("x", "core")
bf16 = jnp.bfloat16
f32 = jnp.float32
VMEM = 48 * 1024 * 1024


def sigmoid(value):
    return 0.5 * jnp.tanh(0.5 * value) + 0.5


def params():
    return pltpu.CompilerParams(vmem_limit_bytes=VMEM)


def row_dot(a, b):
    return lax.dot_general(a, b, (((1,), (1,)), ((), ())), preferred_element_type=f32)


def col_dot(a, b):
    return lax.dot_general(a, b, (((0,), (0,)), ((), ())), preferred_element_type=f32)


def before(parts):
    width = parts[0].shape[1]
    earlier = lax.broadcasted_iota(jnp.int32, (width, width), 0) < lax.broadcasted_iota(
        jnp.int32, (width, width), 1
    )
    inside = jnp.dot(
        jnp.concatenate([part.astype(bf16) for part in parts], axis=0),
        earlier.astype(f32).astype(bf16),
        preferred_element_type=f32,
    )
    high = parts[0].shape[0]
    sums, count = [], jnp.zeros((high, 1), f32)
    for block, part in enumerate(parts):
        sums.append(inside[block * high : (block + 1) * high] + count)
        count = count + jnp.sum(part, axis=1, keepdims=True)
    return sums


def pick(wide, values):
    return jnp.sum(wide * values, axis=0, keepdims=True)


def plan_kernel(owner_ref, local_ref, high_ref, low_ref, target_ref, slot_ref):
    blocks, width = owner_ref.shape
    owners = high_ref.shape[0]
    ids = lax.broadcasted_iota(jnp.int32, (owners, width), 0)
    own = [owner_ref[block : block + 1, :] for block in range(blocks)]
    local = [local_ref[block : block + 1, :] for block in range(blocks)]
    first = [(one == ids).astype(f32) for one in own]
    second = [((one // PIECE) == ids).astype(f32) for one in local]
    free = [jnp.where(one % PIECE < COPIED, 1.0, 0.0) for one in local]
    moved = [jnp.zeros((1, width), f32)] * blocks
    load = sum(jnp.sum(wide, axis=1, keepdims=True) for wide in first)
    for goal in TARGETS:
        excess = jnp.maximum(load - goal, 0.0)
        spare = jnp.maximum(goal - load, 0.0)
        over = [pick(wide, excess) for wide in first]
        room = [pick(wide, spare) for wide in second]
        movable = [
            jnp.where((most > 0.0) & (least > 0.0), one, 0.0)
            for most, least, one in zip(over, room, free)
        ]
        queue = before([wide * one for wide, one in zip(second, movable)])
        kept = [
            jnp.where(pick(wide, sums) < least, one, 0.0)
            for wide, sums, least, one in zip(second, queue, room, movable)
        ]
        gone = before([wide * one for wide, one in zip(first, kept)])
        new = [
            jnp.where(pick(wide, sums) < most, one, 0.0)
            for wide, sums, most, one in zip(first, gone, over, kept)
        ]
        moved = [one + more for one, more in zip(moved, new)]
        free = [one - more for one, more in zip(free, new)]
        change = sum((there - here) * more for here, there, more in zip(first, second, new))
        load = load + jnp.sum(change, axis=1, keepdims=True)
    holder = [here + (there - here) * one for here, there, one in zip(first, second, moved)]
    rank = before(holder)
    slot_ids = lax.broadcasted_iota(jnp.int32, (width, width), 0)
    high_sum = jnp.zeros((owners, width), f32)
    low_sum = jnp.zeros((owners, width), f32)
    widest = jnp.zeros((1, width), jnp.int32)
    for block in range(blocks):
        slot = pick(holder[block], rank[block]).astype(jnp.int32)
        other = moved[block] > 0.0
        row = jnp.where(
            other,
            owners * PIECE + own[block] * PIECE + local[block] % PIECE,
            local[block],
        )
        wide = holder[block].astype(bf16)
        there = (slot == slot_ids).astype(f32)
        high_sum = high_sum + row_dot(wide, (there * (row // DIGIT).astype(f32)).astype(bf16))
        low_sum = low_sum + row_dot(wide, (there * (row % DIGIT).astype(f32)).astype(bf16))
        widest = jnp.maximum(widest, slot)
        target_ref[block : block + 1, :] = jnp.where(other, local[block] // PIECE, own[block])
        slot_ref[block : block + 1, :] = slot
    late = (jnp.max(widest, axis=1, keepdims=True) >= SLOTS).astype(f32)
    last = lax.broadcasted_iota(jnp.int32, (owners, width), 1) == width - 1
    high_ref[...] = jnp.where(last, late, high_sum).astype(bf16)
    low_ref[...] = low_sum.astype(bf16)


def plan(owner, local, owners):
    rows = owner.shape[0]
    blocks = -(-rows // 128)
    spare = blocks * 128 - rows
    owner = jnp.pad(owner[:, 0], (0, spare), constant_values=owners).reshape(blocks, 128)
    local = jnp.pad(local[:, 0], (0, spare)).reshape(blocks, 128)
    high, low, target, slot = pl.pallas_call(
        plan_kernel,
        out_shape=(
            jax.ShapeDtypeStruct((owners, 128), bf16),
            jax.ShapeDtypeStruct((owners, 128), bf16),
            jax.ShapeDtypeStruct((blocks, 128), jnp.int32),
            jax.ShapeDtypeStruct((blocks, 128), jnp.int32),
        ),
        compiler_params=params(),
        name="plan",
    )(owner, local)
    return high, low, target.reshape(-1)[:rows], slot.reshape(-1)[:rows]


def dequantize_kernel(slab_ref, scales_ref, out_ref):
    block = slab_ref.shape[1] // scales_ref.shape[1]
    for part in range(scales_ref.shape[1]):
        lanes = slice(part * block, (part + 1) * block)
        scale = scales_ref[:, part : part + 1].astype(f32)
        out_ref[:, lanes] = (slab_ref[:, lanes].astype(f32) * scale).astype(bf16)


def shares_of(importance):
    return importance / jnp.sum(importance, axis=1, keepdims=True)


def column(values, at):
    lanes = lax.broadcasted_iota(jnp.int32, values.shape, 1)
    return jnp.sum(jnp.where(lanes == at, values, 0.0), axis=1, keepdims=True)


def columns(w_ref, part, start, end):
    return jnp.concatenate(
        [w_ref[2 * part, start:end, :], w_ref[2 * part + 1, start:end, :]], axis=1
    )


def forward_kernel(
    own_ref,
    near_ref,
    importance_ref,
    q_weight_ref,
    q_bias_ref,
    w_far_ref,
    w_bias_ref,
    slope_ref,
    embedded_ref,
    active_ref,
    outer_slope_ref,
    payload_ref,
    pooled,
    w_ref,
    w_arrived,
):
    step = pl.program_id(0)
    w_copy = pltpu.make_async_copy(w_far_ref, w_ref, w_arrived)

    @pl.when(step == 0)
    def _():
        w_copy.start()

    share = column(shares_of(importance_ref[...]), step)
    inner = jnp.dot(near_ref[...], q_weight_ref[...], preferred_element_type=f32) + q_bias_ref[...]
    gate = sigmoid(inner)
    smooth = inner * gate
    slope_ref[...] = (gate + smooth * (1.0 - gate)).astype(bf16)
    term = share * smooth

    @pl.when(step == 0)
    def _():
        pooled[...] = term

    @pl.when(step > 0)
    def _():
        pooled[...] += term

    @pl.when(step == pl.num_programs(0) - 1)
    def _():
        w_copy.wait()
        width = own_ref.shape[1]
        hidden = active_ref.shape[1]
        joined = jnp.concatenate([own_ref[...], pooled[...].astype(bf16)], axis=1)
        outer = jnp.concatenate(
            [
                jnp.dot(joined, columns(w_ref, part, 0, width + hidden), preferred_element_type=f32)
                for part in range(w_ref.shape[0] // 2)
            ],
            axis=1,
        )
        outer = outer + w_bias_ref[...]
        gate = sigmoid(outer)
        active = outer * gate
        active_ref[...] = active
        outer_slope_ref[...] = gate + active * (1.0 - gate)
        scaling = lax.rsqrt(jnp.mean(active * active, axis=1, keepdims=True) + epsilon)
        embedded = (active * scaling).astype(bf16)
        embedded_ref[...] = embedded
        queries = embedded[:PAIRS].astype(f32)
        close = jnp.sum(queries * embedded[PAIRS : 2 * PAIRS].astype(f32), axis=1, keepdims=True)
        close = close / hidden
        first = close.astype(bf16).astype(f32)
        second = (close - first).astype(bf16).astype(f32)
        third = close - first - second
        lanes = lax.broadcasted_iota(jnp.int32, (PAIRS, EXTRA), 1)
        pieces = jnp.where(
            lanes == 0, first, jnp.where(lanes == 1, second, jnp.where(lanes == 2, third, 0.0))
        )
        payload_ref[:PAIRS, :hidden] = embedded[:PAIRS]
        payload_ref[PAIRS:, :hidden] = embedded[2 * PAIRS :]
        payload_ref[:PAIRS, hidden:] = pieces.astype(bf16)
        payload_ref[PAIRS:, hidden:] = jnp.zeros((NEG_DEV, EXTRA), bf16)


def whole(shape):
    return pl.BlockSpec(shape, lambda step: (0,) * len(shape))


def forward(fetched, importance, q_weight, q_bias, w_full, w_bias):
    targets = importance.shape[0]
    width, hidden = q_weight.shape
    sent = PAIRS + NEG_DEV
    return pl.pallas_call(
        forward_kernel,
        grid=(K,),
        in_specs=[
            pl.BlockSpec((targets, width), lambda step: (0, 0)),
            pl.BlockSpec((targets, width), lambda step: (step + 1, 0)),
            whole(importance.shape),
            whole(q_weight.shape),
            whole((1, hidden)),
            pl.BlockSpec(memory_space=pl.ANY),
            whole((1, hidden)),
        ],
        out_specs=[
            pl.BlockSpec((targets, hidden), lambda step: (step, 0)),
            whole((targets, hidden)),
            whole((targets, hidden)),
            whole((targets, hidden)),
            whole((sent, hidden + EXTRA)),
        ],
        out_shape=(
            jax.ShapeDtypeStruct((targets * K, hidden), bf16),
            jax.ShapeDtypeStruct((targets, hidden), bf16),
            jax.ShapeDtypeStruct((targets, hidden), f32),
            jax.ShapeDtypeStruct((targets, hidden), f32),
            jax.ShapeDtypeStruct((sent, hidden + EXTRA), bf16),
        ),
        scratch_shapes=[
            pltpu.VMEM((targets, hidden), f32),
            pltpu.VMEM(w_full.shape, bf16),
            pltpu.SemaphoreType.DMA,
        ],
        compiler_params=params(),
        name="forward",
    )(fetched, fetched, importance, q_weight, q_bias[None, :], w_full, w_bias[None, :])


def backward_kernel(
    fetched_ref,
    importance_ref,
    w_ref,
    slope_ref,
    embedded_ref,
    active_ref,
    outer_slope_ref,
    group_ref,
    grad_ref,
    d_pooled,
    d_inner,
    bias_sum,
    objective_sum,
):
    step = pl.program_id(0)
    targets, hidden = active_ref.shape
    members = group_ref.shape[0]
    negatives_count = members * NEG_DEV

    @pl.when(step == 0)
    def _():
        embedded = embedded_ref[...]
        queries = embedded[:PAIRS]
        positives = embedded[PAIRS : 2 * PAIRS].astype(f32)
        negatives = embedded[2 * PAIRS :]
        group_queries = group_ref[:, :PAIRS, :hidden].reshape(members * PAIRS, hidden)
        group_negatives = group_ref[:, PAIRS:, :hidden].reshape(negatives_count, hidden)
        pieces = group_ref[:, :PAIRS, hidden:].reshape(members * PAIRS, EXTRA).astype(f32)
        group_close = jnp.sum(pieces, axis=1, keepdims=True)
        coef_factor = score_scale / (negatives_count * hidden)
        wide_queries = queries.astype(f32)
        close = jnp.sum(wide_queries * positives, axis=1, keepdims=True) / hidden
        far = row_dot(queries, group_negatives) / hidden
        margins = score_scale * (far - close) + margin
        coef = (sigmoid(margins) * coef_factor).astype(bf16)
        toward = jnp.dot(coef, group_negatives, preferred_element_type=f32)
        row_total = jnp.sum(coef.astype(f32), axis=1, keepdims=True)
        softplus = jnp.maximum(margins, 0.0) + jnp.log1p(jnp.exp(-jnp.abs(margins)))
        objective = jnp.sum(jnp.sum(softplus, axis=1, keepdims=True), axis=0, keepdims=True)
        objective_sum[...] = jnp.broadcast_to(objective / negatives_count, objective_sum.shape)
        group_far = row_dot(group_queries, negatives) / hidden
        group_margins = score_scale * (group_far - group_close) + margin
        group_coef = (sigmoid(group_margins) * coef_factor).astype(bf16)
        d_embed = jnp.concatenate(
            [
                toward - row_total * positives,
                -row_total * wide_queries,
                col_dot(group_coef, group_queries),
            ],
            axis=0,
        )
        active = active_ref[...]
        scaling = lax.rsqrt(jnp.mean(active * active, axis=1, keepdims=True) + epsilon)
        along = jnp.sum(d_embed * active, axis=1, keepdims=True)
        d_active = scaling * (d_embed - active * (along * scaling * scaling / hidden))
        d_outer = (d_active * outer_slope_ref[...]).astype(bf16)
        width = fetched_ref.shape[1]
        pair = 2 * w_ref.shape[2]
        sums = jnp.zeros((targets, hidden), f32)
        for part in range(w_ref.shape[0] // 2):
            lanes = slice(part * pair, (part + 1) * pair)
            sums = sums + row_dot(d_outer[:, lanes], columns(w_ref, part, width, width + hidden))
        d_pooled[...] = sums
        bias_sum[...] = jnp.zeros_like(bias_sum)

    share = column(shares_of(importance_ref[...]), step)
    d_near = (share * d_pooled[...] * slope_ref[...].astype(f32)).astype(bf16)
    d_inner[pl.ds(pl.multiple_of(step * targets, targets), targets), :] = d_near
    bias_sum[...] += jnp.sum(d_near.astype(f32), axis=0, keepdims=True)

    @pl.when(step == pl.num_programs(0) - 1)
    def _():
        near = fetched_ref[targets:, :]
        for part in range(4):
            lanes = slice(part * hidden // 4, (part + 1) * hidden // 4)
            grad_ref[:, lanes] = col_dot(near, d_inner[:, lanes]).astype(bf16)
        grad_ref[:, hidden:] = jnp.zeros((grad_ref.shape[0], EXTRA), bf16)
        rows = lax.broadcasted_iota(jnp.int32, (16, EXTRA), 0)
        small = jnp.zeros((16, EXTRA), f32)
        for part in range(hidden // EXTRA):
            piece = bias_sum[:, part * EXTRA : (part + 1) * EXTRA]
            small = jnp.where(rows == part, piece, small)
        objective = objective_sum[...]
        first = objective.astype(bf16).astype(f32)
        small = jnp.where(rows == hidden // EXTRA, first, small)
        small = jnp.where(rows == hidden // EXTRA + 1, objective - first, small)
        grad_ref[:16, hidden:] = small.astype(bf16)


def backward(fetched, importance, w_full, slope, embedded, active, outer_slope, group):
    targets, hidden = active.shape
    width = fetched.shape[1]
    return pl.pallas_call(
        backward_kernel,
        grid=(K,),
        in_specs=[
            whole(fetched.shape),
            whole(importance.shape),
            whole(w_full.shape),
            pl.BlockSpec((targets, hidden), lambda step: (step, 0)),
            whole(embedded.shape),
            whole(active.shape),
            whole(outer_slope.shape),
            whole(group.shape),
        ],
        out_specs=whole((width, hidden + EXTRA)),
        out_shape=jax.ShapeDtypeStruct((width, hidden + EXTRA), bf16),
        scratch_shapes=[
            pltpu.VMEM((targets, hidden), f32),
            pltpu.VMEM((targets * K, hidden), bf16),
            pltpu.VMEM((1, hidden), f32),
            pltpu.VMEM((1, EXTRA), f32),
        ],
        compiler_params=params(),
        name="backward",
    )(fetched, importance, w_full, slope, embedded, active, outer_slope, group)


def exchange(values, axes):
    return lax.all_to_all(values, axes, split_axis=0, concat_axis=0, tiled=True)


def spread(values, axes):
    count = lax.axis_size(axes)
    return exchange(jnp.broadcast_to(values[None], (count,) + values.shape), axes)


def total(values, axes):
    count = lax.axis_size(axes)
    share = values.shape[0] // count
    parts = exchange(values.reshape((count, share) + values.shape[1:]), axes)
    return jnp.sum(parts.astype(f32), axis=0)


def body(slab, scales, owner, local, importance, q_weight, q_bias, w_weight, w_bias):
    pin_count = lax.axis_size(PIN)
    targets = importance.shape[0]
    width, hidden = q_weight.shape
    high, low, target, slot = plan(owner, local, pin_count)
    ready = pl.pallas_call(
        dequantize_kernel,
        out_shape=jax.ShapeDtypeStruct(slab.shape, bf16),
        compiler_params=params(),
        name="dequantize",
    )(slab, scales)
    members = lax.axis_size(GRP)
    lanes = hidden // members
    rows = w_weight.shape[0]
    mine = lax.dynamic_slice_in_dim(w_weight, lax.axis_index(GRP) * lanes, lanes, 1)
    tail = jnp.broadcast_to(mine[PIECE:].reshape(1, 2, width), (pin_count, 2, width))
    ids = jnp.pad(jnp.concatenate([high, low], axis=1), ((0, 0), (0, width - 256)))
    tail = jnp.concatenate([tail, jnp.pad(ids[:, None], ((0, 0), (0, 1), (0, 0)))], axis=1)
    sent = jnp.concatenate([ready.reshape(pin_count, PIECE, width)[:, :COPIED], tail], axis=1)
    side = jnp.broadcast_to(mine[None, :PIECE], (pin_count, PIECE, lanes))
    sent = exchange(jnp.concatenate([sent, side], axis=2), PIN)
    table = sent[:, :, :width].reshape(pin_count * PIECE, width)
    table = jnp.concatenate([ready, table], axis=0)
    ids = sent[:, COPIED + 2].astype(jnp.int32)
    asked = ids[:, :ALL_SLOTS] * DIGIT + ids[:, 128 : 128 + ALL_SLOTS]
    picked = jnp.take(table, asked[:, :SLOTS].reshape(-1), axis=0, mode="clip")
    got = exchange(picked.reshape(pin_count, SLOTS, width), PIN).reshape(-1, width)
    w_part = sent[:, COPIED : COPIED + 2, :width].reshape(pin_count, rows - PIECE, lanes)
    w_part = jnp.concatenate([sent[:, :, width:], w_part], axis=1)
    w_part = w_part.reshape(pin_count * rows, lanes)
    over = jnp.max(sent[:, COPIED + 2, 127])
    w_part = jnp.concatenate([w_part, jnp.broadcast_to(over, (16, lanes))], axis=0)
    w_full = lax.all_gather(w_part, GRP, axis=0, tiled=False)
    over = jnp.max(w_full[:, -16:, :].astype(f32)) > 0.5

    def ordered(values):
        return values.reshape(targets, K + 1).T.reshape(-1)

    target, slot = ordered(target), ordered(slot)
    late = slot >= SLOTS
    fetched = jnp.take(got, jnp.where(late, 0, target * SLOTS + slot), axis=0, mode="clip")

    def second_exchange(fetched):
        more = ALL_SLOTS - SLOTS
        picked = jnp.take(table, asked[:, SLOTS:].reshape(-1), axis=0, mode="clip")
        got = exchange(picked.reshape(pin_count, more, width), PIN).reshape(-1, width)
        place = jnp.where(late, target * more + slot - SLOTS, 0)
        return jnp.where(late[:, None], jnp.take(got, place, axis=0, mode="clip"), fetched)

    fetched = lax.cond(over, second_exchange, lambda fetched: fetched, fetched)
    slope, embedded, active, outer_slope, payload = forward(
        fetched, importance, q_weight, q_bias, w_full, w_bias
    )
    group = spread(spread(payload, "x"), "core")
    group = group.reshape((-1,) + payload.shape)
    grads = backward(fetched, importance, w_full, slope, embedded, active, outer_slope, group)
    grads = total(grads, "core").astype(bf16)
    grads = total(grads, PIN)
    grads = jnp.sum(spread(grads, "x"), axis=0)
    loss_row = hidden // EXTRA
    grads = spread(grads.astype(bf16), PIN).reshape(-1, hidden + EXTRA)
    grads = spread(grads, "core").reshape(-1, hidden + EXTRA)
    grad_q = grads[:, :hidden].astype(f32)
    grad_bias = grads[:loss_row, hidden:].astype(f32).reshape(-1)
    objective = jnp.sum(grads[loss_row : loss_row + 2, hidden].astype(f32))
    devices = pin_count * lax.axis_size(GRP)
    loss = objective / (PAIRS * devices)
    return (embedded, grad_q, grad_bias, loss)


def solution(mesh):
    devices = mesh.devices.reshape(8, 8, 4, 2)
    fine = Mesh(devices, PIN + GRP)
    in_specs = (
        P(PIN, None),
        P(PIN, None),
        P(PIN + GRP, None),
        P(PIN + GRP, None),
        P(PIN + GRP, None),
        P(),
        P(),
        P(PIN, None),
        P(),
    )
    out_specs = (P(PIN + GRP, None), P(), P(), P())
    return jax.shard_map(body, mesh=fine, in_specs=in_specs, out_specs=out_specs, check_vma=False)
```

```python
import jax
import jax.numpy as jnp
from jax import lax
from jax.experimental import pallas as pl
from jax.experimental.pallas import tpu as pltpu
from jax.sharding import Mesh
from jax.sharding import PartitionSpec as P

K = 10
PAIRS = 64
NEG_DEV = 64
SLOTS = 40
ALL_SLOTS = 80
PIECE = 16
COPIED = 12
TARGETS = (42, 34, 38, 36, 40, 38, 40, 40)
DIGIT = 32
PER = 5
CHUNK = 256
EXTRA = 128

margin = 0.5
score_scale = 8.0
epsilon = 1e-05

PIN = ("y", "z")
GRP = ("x", "core")
bf16 = jnp.bfloat16
f32 = jnp.float32


def sigmoid(value):
    return 0.5 * jnp.tanh(0.5 * value) + 0.5


def params(megabytes=24):
    return pltpu.CompilerParams(vmem_limit_bytes=megabytes * 1024 * 1024)


def row_dot(a, b):
    return lax.dot_general(a, b, (((1,), (1,)), ((), ())), preferred_element_type=f32)


def col_dot(a, b):
    return lax.dot_general(a, b, (((0,), (0,)), ((), ())), preferred_element_type=f32)


def before(parts):
    width = parts[0].shape[1]
    earlier = lax.broadcasted_iota(jnp.int32, (width, width), 0) < lax.broadcasted_iota(
        jnp.int32, (width, width), 1
    )
    inside = jnp.dot(
        jnp.concatenate([part.astype(bf16) for part in parts], axis=0),
        earlier.astype(f32).astype(bf16),
        preferred_element_type=f32,
    )
    high = parts[0].shape[0]
    sums, count = [], jnp.zeros((high, 1), f32)
    for block, part in enumerate(parts):
        sums.append(inside[block * high : (block + 1) * high] + count)
        count = count + jnp.sum(part, axis=1, keepdims=True)
    return sums


def pick(wide, values):
    return jnp.sum(wide * values, axis=0, keepdims=True)


def plan_kernel(owner_ref, local_ref, high_ref, low_ref, target_ref, slot_ref):
    blocks, width = owner_ref.shape
    owners = high_ref.shape[0]
    ids = lax.broadcasted_iota(jnp.int32, (owners, width), 0)
    own = [owner_ref[block : block + 1, :] for block in range(blocks)]
    local = [local_ref[block : block + 1, :] for block in range(blocks)]
    first = [(one == ids).astype(f32) for one in own]
    second = [((one // PIECE) == ids).astype(f32) for one in local]
    free = [jnp.where(one % PIECE < COPIED, 1.0, 0.0) for one in local]
    moved = [jnp.zeros((1, width), f32)] * blocks
    load = sum(jnp.sum(wide, axis=1, keepdims=True) for wide in first)
    for goal in TARGETS:
        excess = jnp.maximum(load - goal, 0.0)
        spare = jnp.maximum(goal - load, 0.0)
        over = [pick(wide, excess) for wide in first]
        room = [pick(wide, spare) for wide in second]
        movable = [
            jnp.where((most > 0.0) & (least > 0.0), one, 0.0)
            for most, least, one in zip(over, room, free)
        ]
        queue = before([wide * one for wide, one in zip(second, movable)])
        kept = [
            jnp.where(pick(wide, sums) < least, one, 0.0)
            for wide, sums, least, one in zip(second, queue, room, movable)
        ]
        gone = before([wide * one for wide, one in zip(first, kept)])
        new = [
            jnp.where(pick(wide, sums) < most, one, 0.0)
            for wide, sums, most, one in zip(first, gone, over, kept)
        ]
        moved = [one + more for one, more in zip(moved, new)]
        free = [one - more for one, more in zip(free, new)]
        change = sum((there - here) * more for here, there, more in zip(first, second, new))
        load = load + jnp.sum(change, axis=1, keepdims=True)
    holder = [here + (there - here) * one for here, there, one in zip(first, second, moved)]
    rank = before(holder)
    slot_ids = lax.broadcasted_iota(jnp.int32, (width, width), 0)
    high_sum = jnp.zeros((owners, width), f32)
    low_sum = jnp.zeros((owners, width), f32)
    widest = jnp.zeros((1, width), jnp.int32)
    for block in range(blocks):
        slot = pick(holder[block], rank[block]).astype(jnp.int32)
        other = moved[block] > 0.0
        row = jnp.where(
            other,
            owners * PIECE + own[block] * PIECE + local[block] % PIECE,
            local[block],
        )
        wide = holder[block].astype(bf16)
        there = (slot == slot_ids).astype(f32)
        high_sum = high_sum + row_dot(wide, (there * (row // DIGIT).astype(f32)).astype(bf16))
        low_sum = low_sum + row_dot(wide, (there * (row % DIGIT).astype(f32)).astype(bf16))
        widest = jnp.maximum(widest, slot)
        target_ref[block : block + 1, :] = jnp.where(other, local[block] // PIECE, own[block])
        slot_ref[block : block + 1, :] = slot
    late = (jnp.max(widest, axis=1, keepdims=True) >= SLOTS).astype(f32)
    last = lax.broadcasted_iota(jnp.int32, (owners, width), 1) == width - 1
    high_ref[...] = jnp.where(last, late, high_sum).astype(bf16)
    low_ref[...] = low_sum.astype(bf16)


def plan(owner, local, owners):
    rows = owner.shape[0]
    blocks = -(-rows // 128)
    spare = blocks * 128 - rows
    owner = jnp.pad(owner[:, 0], (0, spare), constant_values=owners).reshape(blocks, 128)
    local = jnp.pad(local[:, 0], (0, spare)).reshape(blocks, 128)
    high, low, target, slot = pl.pallas_call(
        plan_kernel,
        out_shape=(
            jax.ShapeDtypeStruct((owners, 128), bf16),
            jax.ShapeDtypeStruct((owners, 128), bf16),
            jax.ShapeDtypeStruct((blocks, 128), jnp.int32),
            jax.ShapeDtypeStruct((blocks, 128), jnp.int32),
        ),
        compiler_params=params(),
        name="plan",
    )(owner, local)
    return high, low, target.reshape(-1)[:rows], slot.reshape(-1)[:rows]


def dequantize_kernel(slab_ref, scales_ref, out_ref):
    block = slab_ref.shape[1] // scales_ref.shape[1]
    for part in range(scales_ref.shape[1]):
        lanes = slice(part * block, (part + 1) * block)
        scale = scales_ref[:, part : part + 1].astype(f32)
        out_ref[:, lanes] = (slab_ref[:, lanes].astype(f32) * scale).astype(bf16)


def shares_of(importance):
    return importance / jnp.sum(importance, axis=1, keepdims=True)


def column(values, at):
    lanes = lax.broadcasted_iota(jnp.int32, values.shape, 1)
    return jnp.sum(jnp.where(lanes == at, values, 0.0), axis=1, keepdims=True)


def columns(w_ref, part, start, end):
    return jnp.concatenate(
        [w_ref[2 * part, start:end, :], w_ref[2 * part + 1, start:end, :]], axis=1
    )


def forward_kernel(
    own_ref,
    near_ref,
    importance_ref,
    q_weight_ref,
    q_bias_ref,
    w_far_ref,
    w_bias_ref,
    slope_ref,
    embedded_ref,
    active_ref,
    outer_slope_ref,
    payload_ref,
    pooled,
    w_ref,
    w_arrived,
):
    step = pl.program_id(0)
    w_copy = pltpu.make_async_copy(w_far_ref, w_ref, w_arrived)

    @pl.when(step == 0)
    def _():
        w_copy.start()

    targets = pooled.shape[0]
    shares = shares_of(importance_ref[...])
    share = [column(shares, step * PER + at) for at in range(PER)]

    @pl.when(step == 0)
    def _():
        pooled[...] = jnp.zeros_like(pooled)

    for part in range(pooled.shape[1] // CHUNK):
        lanes = slice(part * CHUNK, (part + 1) * CHUNK)
        inner = jnp.dot(near_ref[...], q_weight_ref[:, lanes], preferred_element_type=f32)
        inner = inner + q_bias_ref[:, lanes]
        gate = sigmoid(inner)
        smooth = inner * gate
        slope_ref[:, lanes] = (gate + smooth * (1.0 - gate)).astype(bf16)
        total_term = pooled[:, lanes]
        for at in range(PER):
            total_term = total_term + share[at] * smooth[at * targets : (at + 1) * targets]
        pooled[:, lanes] = total_term

    @pl.when(step == pl.num_programs(0) - 1)
    def _():
        w_copy.wait()
        width = own_ref.shape[1]
        hidden = active_ref.shape[1]
        joined = jnp.concatenate([own_ref[...], pooled[...].astype(bf16)], axis=1)
        outer = jnp.concatenate(
            [
                jnp.dot(joined, columns(w_ref, part, 0, width + hidden), preferred_element_type=f32)
                for part in range(w_ref.shape[0] // 2)
            ],
            axis=1,
        )
        outer = outer + w_bias_ref[...]
        gate = sigmoid(outer)
        active = outer * gate
        active_ref[...] = active
        outer_slope_ref[...] = gate + active * (1.0 - gate)
        scaling = lax.rsqrt(jnp.mean(active * active, axis=1, keepdims=True) + epsilon)
        embedded = (active * scaling).astype(bf16)
        embedded_ref[...] = embedded
        queries = embedded[:PAIRS].astype(f32)
        close = jnp.sum(queries * embedded[PAIRS : 2 * PAIRS].astype(f32), axis=1, keepdims=True)
        close = close / hidden
        first = close.astype(bf16).astype(f32)
        second = (close - first).astype(bf16).astype(f32)
        third = close - first - second
        lanes = lax.broadcasted_iota(jnp.int32, (PAIRS, EXTRA), 1)
        pieces = jnp.where(
            lanes == 0, first, jnp.where(lanes == 1, second, jnp.where(lanes == 2, third, 0.0))
        )
        payload_ref[:PAIRS, :hidden] = embedded[:PAIRS]
        payload_ref[PAIRS:, :hidden] = embedded[2 * PAIRS :]
        payload_ref[:PAIRS, hidden:] = pieces.astype(bf16)
        payload_ref[PAIRS:, hidden:] = jnp.zeros((NEG_DEV, EXTRA), bf16)


def whole(shape):
    return pl.BlockSpec(shape, lambda step: (0,) * len(shape))


def forward(fetched, importance, q_weight, q_bias, w_full, w_bias):
    targets = importance.shape[0]
    width, hidden = q_weight.shape
    sent = PAIRS + NEG_DEV
    return pl.pallas_call(
        forward_kernel,
        grid=(K // PER,),
        in_specs=[
            pl.BlockSpec((targets, width), lambda step: (K, 0)),
            pl.BlockSpec((targets * PER, width), lambda step: (step, 0)),
            whole(importance.shape),
            whole(q_weight.shape),
            whole((1, hidden)),
            pl.BlockSpec(memory_space=pl.ANY),
            whole((1, hidden)),
        ],
        out_specs=[
            pl.BlockSpec((targets * PER, hidden), lambda step: (step, 0)),
            whole((targets, hidden)),
            whole((targets, hidden)),
            whole((targets, hidden)),
            whole((sent, hidden + EXTRA)),
        ],
        out_shape=(
            jax.ShapeDtypeStruct((targets * K, hidden), bf16),
            jax.ShapeDtypeStruct((targets, hidden), bf16),
            jax.ShapeDtypeStruct((targets, hidden), f32),
            jax.ShapeDtypeStruct((targets, hidden), f32),
            jax.ShapeDtypeStruct((sent, hidden + EXTRA), bf16),
        ),
        scratch_shapes=[
            pltpu.VMEM((targets, hidden), f32),
            pltpu.VMEM(w_full.shape, bf16),
            pltpu.SemaphoreType.DMA,
        ],
        compiler_params=params(),
        name="forward",
    )(fetched, fetched, importance, q_weight, q_bias[None, :], w_full, w_bias[None, :])


def backward_kernel(
    fetched_ref,
    importance_ref,
    w_far_ref,
    slope_far_ref,
    embedded_ref,
    active_ref,
    outer_slope_ref,
    group_ref,
    grad_ref,
    d_inner,
    w_ref,
    w_arrived,
    slope_ref,
    slope_arrived,
):
    w_copy = pltpu.make_async_copy(w_far_ref, w_ref, w_arrived)
    slope_copy = pltpu.make_async_copy(slope_far_ref, slope_ref, slope_arrived)
    w_copy.start()
    slope_copy.start()
    targets, hidden = active_ref.shape
    members = group_ref.shape[0]
    negatives_count = members * NEG_DEV

    embedded = embedded_ref[...]
    queries = embedded[:PAIRS]
    positives = embedded[PAIRS : 2 * PAIRS].astype(f32)
    negatives = embedded[2 * PAIRS :]
    group_queries = group_ref[:, :PAIRS, :hidden].reshape(members * PAIRS, hidden)
    group_negatives = group_ref[:, PAIRS:, :hidden].reshape(negatives_count, hidden)
    pieces = group_ref[:, :PAIRS, hidden:].reshape(members * PAIRS, EXTRA).astype(f32)
    group_close = jnp.sum(pieces, axis=1, keepdims=True)
    coef_factor = score_scale / (negatives_count * hidden)
    wide_queries = queries.astype(f32)
    close = jnp.sum(wide_queries * positives, axis=1, keepdims=True) / hidden
    far = row_dot(queries, group_negatives) / hidden
    margins = score_scale * (far - close) + margin
    coef = (sigmoid(margins) * coef_factor).astype(bf16)
    toward = jnp.dot(coef, group_negatives, preferred_element_type=f32)
    row_total = jnp.sum(coef.astype(f32), axis=1, keepdims=True)
    softplus = jnp.maximum(margins, 0.0) + jnp.log1p(jnp.exp(-jnp.abs(margins)))
    objective = jnp.sum(jnp.sum(softplus, axis=1, keepdims=True), axis=0, keepdims=True)
    objective = objective / negatives_count
    group_far = row_dot(group_queries, negatives) / hidden
    group_margins = score_scale * (group_far - group_close) + margin
    group_coef = (sigmoid(group_margins) * coef_factor).astype(bf16)
    d_embed = jnp.concatenate(
        [
            toward - row_total * positives,
            -row_total * wide_queries,
            col_dot(group_coef, group_queries),
        ],
        axis=0,
    )
    active = active_ref[...]
    scaling = lax.rsqrt(jnp.mean(active * active, axis=1, keepdims=True) + epsilon)
    along = jnp.sum(d_embed * active, axis=1, keepdims=True)
    d_active = scaling * (d_embed - active * (along * scaling * scaling / hidden))
    d_outer = (d_active * outer_slope_ref[...]).astype(bf16)
    w_copy.wait()
    width = fetched_ref.shape[1]
    pair = 2 * w_ref.shape[2]
    sums = jnp.zeros((targets, hidden), f32)
    for part in range(w_ref.shape[0] // 2):
        lanes = slice(part * pair, (part + 1) * pair)
        sums = sums + row_dot(d_outer[:, lanes], columns(w_ref, part, width, width + hidden))
    d_pooled = sums

    shares = shares_of(importance_ref[...])
    sums = jnp.zeros((1, hidden), f32)
    slope_copy.wait()
    for at in range(K):
        rows = slice(at * targets, (at + 1) * targets)
        d_near = (column(shares, at) * d_pooled * slope_ref[rows, :].astype(f32)).astype(bf16)
        d_inner[rows, :] = d_near
        sums = sums + jnp.sum(d_near.astype(f32), axis=0, keepdims=True)

    near = fetched_ref[: K * targets, :]
    grad_ref[:, :hidden] = col_dot(near, d_inner[...]).astype(bf16)
    grad_ref[:, hidden:] = jnp.zeros((grad_ref.shape[0], EXTRA), bf16)
    rows = lax.broadcasted_iota(jnp.int32, (16, EXTRA), 0)
    small = jnp.zeros((16, EXTRA), f32)
    for part in range(hidden // EXTRA):
        piece = sums[:, part * EXTRA : (part + 1) * EXTRA]
        small = jnp.where(rows == part, piece, small)
    first = objective.astype(bf16).astype(f32)
    small = jnp.where(rows == hidden // EXTRA, first, small)
    small = jnp.where(rows == hidden // EXTRA + 1, objective - first, small)
    grad_ref[:16, hidden:] = small.astype(bf16)


def backward(fetched, importance, w_full, slope, embedded, active, outer_slope, group):
    targets, hidden = active.shape
    width = fetched.shape[1]
    far = pl.BlockSpec(memory_space=pl.ANY)
    near = pl.BlockSpec(memory_space=pltpu.VMEM)
    return pl.pallas_call(
        backward_kernel,
        in_specs=[near, near, far, far, near, near, near, near],
        out_specs=near,
        out_shape=jax.ShapeDtypeStruct((width, hidden + EXTRA), bf16),
        scratch_shapes=[
            pltpu.VMEM((targets * K, hidden), bf16),
            pltpu.VMEM(w_full.shape, bf16),
            pltpu.SemaphoreType.DMA,
            pltpu.VMEM(slope.shape, bf16),
            pltpu.SemaphoreType.DMA,
        ],
        compiler_params=params(36),
        name="backward",
    )(fetched, importance, w_full, slope, embedded, active, outer_slope, group)


def exchange(values, axes):
    return lax.all_to_all(values, axes, split_axis=0, concat_axis=0, tiled=True)


def spread(values, axes):
    count = lax.axis_size(axes)
    return exchange(jnp.broadcast_to(values[None], (count,) + values.shape), axes)


def total(values, axes):
    count = lax.axis_size(axes)
    share = values.shape[0] // count
    parts = exchange(values.reshape((count, share) + values.shape[1:]), axes)
    return jnp.sum(parts.astype(f32), axis=0)


def body(slab, scales, owner, local, importance, q_weight, q_bias, w_weight, w_bias):
    pin_count = lax.axis_size(PIN)
    targets = importance.shape[0]
    width, hidden = q_weight.shape
    high, low, target, slot = plan(owner, local, pin_count)
    ready = pl.pallas_call(
        dequantize_kernel,
        out_shape=jax.ShapeDtypeStruct(slab.shape, bf16),
        compiler_params=params(),
        name="dequantize",
    )(slab, scales)
    members = lax.axis_size(GRP)
    lanes = hidden // members
    rows = w_weight.shape[0]
    mine = lax.dynamic_slice_in_dim(w_weight, lax.axis_index(GRP) * lanes, lanes, 1)
    tail = jnp.broadcast_to(mine[PIECE:].reshape(1, 2, width), (pin_count, 2, width))
    ids = jnp.pad(jnp.concatenate([high, low], axis=1), ((0, 0), (0, width - 256)))
    tail = jnp.concatenate([tail, jnp.pad(ids[:, None], ((0, 0), (0, 1), (0, 0)))], axis=1)
    sent = jnp.concatenate([ready.reshape(pin_count, PIECE, width)[:, :COPIED], tail], axis=1)
    side = jnp.broadcast_to(mine[None, :PIECE], (pin_count, PIECE, lanes))
    sent = exchange(jnp.concatenate([sent, side], axis=2), PIN)
    table = sent[:, :, :width].reshape(pin_count * PIECE, width)
    table = jnp.concatenate([ready, table], axis=0)
    ids = sent[:, COPIED + 2].astype(jnp.int32)
    asked = ids[:, :ALL_SLOTS] * DIGIT + ids[:, 128 : 128 + ALL_SLOTS]
    picked = jnp.take(table, asked[:, :SLOTS].reshape(-1), axis=0, mode="clip")
    got = exchange(picked.reshape(pin_count, SLOTS, width), PIN).reshape(-1, width)
    w_part = sent[:, COPIED : COPIED + 2, :width].reshape(pin_count, rows - PIECE, lanes)
    w_part = jnp.concatenate([sent[:, :, width:], w_part], axis=1)
    w_part = w_part.reshape(pin_count * rows, lanes)
    over = jnp.max(sent[:, COPIED + 2, 127])
    w_part = jnp.concatenate([w_part, jnp.broadcast_to(over, (16, lanes))], axis=0)
    w_full = lax.all_gather(w_part, GRP, axis=0, tiled=False)
    over = jnp.max(w_full[:, -1, :1].astype(f32)) > 0.5

    def ordered(values):
        return jnp.roll(values.reshape(targets, K + 1).T, -1, axis=0).reshape(-1)

    target, slot = ordered(target), ordered(slot)
    late = slot >= SLOTS
    fetched = jnp.take(got, jnp.where(late, 0, target * SLOTS + slot), axis=0, mode="clip")

    def second_exchange(fetched):
        more = ALL_SLOTS - SLOTS
        picked = jnp.take(table, asked[:, SLOTS:].reshape(-1), axis=0, mode="clip")
        got = exchange(picked.reshape(pin_count, more, width), PIN).reshape(-1, width)
        place = jnp.where(late, target * more + slot - SLOTS, 0)
        return jnp.where(late[:, None], jnp.take(got, place, axis=0, mode="clip"), fetched)

    fetched = lax.cond(over, second_exchange, lambda fetched: fetched, fetched)
    slope, embedded, active, outer_slope, payload = forward(
        fetched, importance, q_weight, q_bias, w_full, w_bias
    )
    group = spread(spread(payload, "x"), "core")
    group = group.reshape((-1,) + payload.shape)
    grads = backward(fetched, importance, w_full, slope, embedded, active, outer_slope, group)
    grads = total(grads, "core").astype(bf16)
    grads = total(grads, PIN)
    grads = jnp.sum(spread(grads, "x"), axis=0)
    loss_row = hidden // EXTRA
    grads = spread(grads.astype(bf16), PIN).reshape(-1, hidden + EXTRA)
    grads = spread(grads, "core").reshape(-1, hidden + EXTRA)
    grad_q = grads[:, :hidden].astype(f32)
    grad_bias = grads[:loss_row, hidden:].astype(f32).reshape(-1)
    objective = jnp.sum(grads[loss_row : loss_row + 2, hidden].astype(f32))
    devices = pin_count * lax.axis_size(GRP)
    loss = objective / (PAIRS * devices)
    return (embedded, grad_q, grad_bias, loss)


def solution(mesh):
    devices = mesh.devices.reshape(8, 8, 4, 2)
    fine = Mesh(devices, PIN + GRP)
    in_specs = (
        P(PIN, None),
        P(PIN, None),
        P(PIN + GRP, None),
        P(PIN + GRP, None),
        P(PIN + GRP, None),
        P(),
        P(),
        P(PIN, None),
        P(),
    )
    out_specs = (P(PIN + GRP, None), P(), P(), P())
    return jax.shard_map(body, mesh=fine, in_specs=in_specs, out_specs=out_specs, check_vma=False)
```

```python
import jax
import jax.numpy as jnp
from jax import lax
from jax.experimental import pallas as pl
from jax.experimental.pallas import tpu as pltpu
from jax.sharding import Mesh
from jax.sharding import PartitionSpec as P

K = 10
PAIRS = 64
NEG_DEV = 64
SLOTS = 40
ALL_SLOTS = 80
PIECE = 16
COPIED = 12
TARGETS = (42, 34, 38, 36, 40, 38, 40, 40)
DIGIT = 32
PER = 5
CHUNK = 256
EXTRA = 128

margin = 0.5
score_scale = 8.0
epsilon = 1e-05

PIN = ("y", "z")
GRP = ("x", "core")
bf16 = jnp.bfloat16
f32 = jnp.float32


def sigmoid(value):
    return 0.5 * jnp.tanh(0.5 * value) + 0.5


def params(megabytes=24):
    return pltpu.CompilerParams(vmem_limit_bytes=megabytes * 1024 * 1024)


def row_dot(a, b):
    return lax.dot_general(a, b, (((1,), (1,)), ((), ())), preferred_element_type=f32)


def col_dot(a, b):
    return lax.dot_general(a, b, (((0,), (0,)), ((), ())), preferred_element_type=f32)


def before(parts):
    width = parts[0].shape[1]
    earlier = lax.broadcasted_iota(jnp.int32, (width, width), 0) < lax.broadcasted_iota(
        jnp.int32, (width, width), 1
    )
    inside = jnp.dot(
        jnp.concatenate([part.astype(bf16) for part in parts], axis=0),
        earlier.astype(f32).astype(bf16),
        preferred_element_type=f32,
    )
    high = parts[0].shape[0]
    sums, count = [], jnp.zeros((high, 1), f32)
    for block, part in enumerate(parts):
        sums.append(inside[block * high : (block + 1) * high] + count)
        count = count + jnp.sum(part, axis=1, keepdims=True)
    return sums


def pick(wide, values):
    return jnp.sum(wide * values, axis=0, keepdims=True)


def plan_kernel(
    row_ref,
    slab_far_ref,
    scales_ref,
    w_ref,
    sent_ref,
    ready_ref,
    target_ref,
    slot_ref,
    slab_ref,
    slab_arrived,
):
    slab_copy = pltpu.make_async_copy(slab_far_ref, slab_ref, slab_arrived)
    slab_copy.start()
    blocks, width = row_ref.shape
    pins = ready_ref.shape[0]
    owners = pins // PIECE
    ids = lax.broadcasted_iota(jnp.int32, (owners, width), 0)
    own = [row_ref[block : block + 1, :] // pins for block in range(blocks)]
    local = [row_ref[block : block + 1, :] % pins for block in range(blocks)]
    first = [(one == ids).astype(f32) for one in own]
    second = [((one // PIECE) == ids).astype(f32) for one in local]
    free = [jnp.where(one % PIECE < COPIED, 1.0, 0.0) for one in local]
    moved = [jnp.zeros((1, width), f32)] * blocks
    load = sum(jnp.sum(wide, axis=1, keepdims=True) for wide in first)
    for goal in TARGETS:
        excess = jnp.maximum(load - goal, 0.0)
        spare = jnp.maximum(goal - load, 0.0)
        over = [pick(wide, excess) for wide in first]
        room = [pick(wide, spare) for wide in second]
        movable = [
            jnp.where((most > 0.0) & (least > 0.0), one, 0.0)
            for most, least, one in zip(over, room, free)
        ]
        queue = before([wide * one for wide, one in zip(second, movable)])
        kept = [
            jnp.where(pick(wide, sums) < least, one, 0.0)
            for wide, sums, least, one in zip(second, queue, room, movable)
        ]
        gone = before([wide * one for wide, one in zip(first, kept)])
        new = [
            jnp.where(pick(wide, sums) < most, one, 0.0)
            for wide, sums, most, one in zip(first, gone, over, kept)
        ]
        moved = [one + more for one, more in zip(moved, new)]
        free = [one - more for one, more in zip(free, new)]
        change = sum((there - here) * more for here, there, more in zip(first, second, new))
        load = load + jnp.sum(change, axis=1, keepdims=True)
    holder = [here + (there - here) * one for here, there, one in zip(first, second, moved)]
    rank = before(holder)
    slot_ids = lax.broadcasted_iota(jnp.int32, (width, width), 0)
    high_sum = jnp.zeros((owners, width), f32)
    low_sum = jnp.zeros((owners, width), f32)
    widest = jnp.zeros((1, width), jnp.int32)
    for block in range(blocks):
        slot = pick(holder[block], rank[block]).astype(jnp.int32)
        other = moved[block] > 0.0
        row = jnp.where(
            other,
            owners * PIECE + own[block] * PIECE + local[block] % PIECE,
            local[block],
        )
        wide = holder[block].astype(bf16)
        there = (slot == slot_ids).astype(f32)
        high_sum = high_sum + row_dot(wide, (there * (row // DIGIT).astype(f32)).astype(bf16))
        low_sum = low_sum + row_dot(wide, (there * (row % DIGIT).astype(f32)).astype(bf16))
        widest = jnp.maximum(widest, slot)
        target_ref[block : block + 1, :] = jnp.where(other, local[block] // PIECE, own[block])
        slot_ref[block : block + 1, :] = slot
    late = (jnp.max(widest, axis=1, keepdims=True) >= SLOTS).astype(f32)
    last = lax.broadcasted_iota(jnp.int32, (owners, width), 1) == width - 1
    digits = jnp.concatenate([jnp.where(last, late, high_sum), low_sum], axis=1).astype(bf16)
    slab_copy.wait()
    block = slab_ref.shape[1] // scales_ref.shape[1]
    for part in range(scales_ref.shape[1]):
        lanes = slice(part * block, (part + 1) * block)
        scale = scales_ref[:, part : part + 1].astype(f32)
        ready_ref[:, lanes] = (slab_ref[:, lanes].astype(f32) * scale).astype(bf16)
    here = COPIED + 2
    piece_row = lax.broadcasted_iota(jnp.int32, (pins, owners), 1) * PIECE + here
    rows = lax.broadcasted_iota(jnp.int32, (pins, owners), 0)
    digits = jnp.dot(
        (rows == piece_row).astype(f32).astype(bf16), digits, preferred_element_type=f32
    )
    place = lax.broadcasted_iota(jnp.int32, (pins, block), 0) % PIECE
    w_part = w_ref[...].astype(f32)
    for part in range(scales_ref.shape[1]):
        lanes = slice(part * block, (part + 1) * block)
        values = ready_ref[:, lanes].astype(f32)
        values = jnp.where(place == COPIED, w_part[PIECE + part : PIECE + part + 1], values)
        values = jnp.where(place == COPIED + 1, w_part[PIECE + 4 + part : PIECE + 5 + part], values)
        if part < 2:
            values = jnp.where(place == here, digits[:, lanes], values)
        sent_ref[:, lanes] = values.astype(bf16)
    side = jnp.broadcast_to(w_part[None, :PIECE], (owners, PIECE, block)).reshape(pins, block)
    sent_ref[:, scales_ref.shape[1] * block :] = side.astype(bf16)


def plan(slab, scales, w_part, owner, local, owners):
    rows = owner.shape[0]
    pins = slab.shape[0]
    blocks = -(-rows // 128)
    spare = blocks * 128 - rows
    row = (owner * pins + local)[:, 0]
    row = jnp.pad(row, (0, spare), constant_values=owners * pins).reshape(blocks, 128)
    near = pl.BlockSpec(memory_space=pltpu.VMEM)
    sent, ready, target, slot = pl.pallas_call(
        plan_kernel,
        in_specs=[near, pl.BlockSpec(memory_space=pl.ANY), near, near],
        out_shape=(
            jax.ShapeDtypeStruct((pins, slab.shape[1] + w_part.shape[1]), bf16),
            jax.ShapeDtypeStruct(slab.shape, bf16),
            jax.ShapeDtypeStruct((blocks, 128), jnp.int32),
            jax.ShapeDtypeStruct((blocks, 128), jnp.int32),
        ),
        scratch_shapes=[pltpu.VMEM(slab.shape, bf16), pltpu.SemaphoreType.DMA],
        compiler_params=params(),
        name="plan",
    )(row, slab, scales, w_part)
    return sent, ready, target.reshape(-1)[:rows], slot.reshape(-1)[:rows]


def shares_of(importance):
    return importance / jnp.sum(importance, axis=1, keepdims=True)


def column(values, at):
    lanes = lax.broadcasted_iota(jnp.int32, values.shape, 1)
    return jnp.sum(jnp.where(lanes == at, values, 0.0), axis=1, keepdims=True)


def columns(w_ref, part, start, end):
    return jnp.concatenate(
        [w_ref[2 * part, start:end, :], w_ref[2 * part + 1, start:end, :]], axis=1
    )


def forward_kernel(
    own_ref,
    near_ref,
    importance_ref,
    q_weight_ref,
    q_bias_ref,
    w_far_ref,
    w_bias_ref,
    slope_ref,
    embedded_ref,
    active_ref,
    outer_slope_ref,
    payload_ref,
    pooled,
    w_ref,
    w_arrived,
):
    step = pl.program_id(0)
    w_copy = pltpu.make_async_copy(w_far_ref, w_ref, w_arrived)

    @pl.when(step == 0)
    def _():
        w_copy.start()

    targets = pooled.shape[0]
    shares = shares_of(importance_ref[...])
    share = [column(shares, step * PER + at) for at in range(PER)]

    @pl.when(step == 0)
    def _():
        pooled[...] = jnp.zeros_like(pooled)

    for part in range(pooled.shape[1] // CHUNK):
        lanes = slice(part * CHUNK, (part + 1) * CHUNK)
        inner = jnp.dot(near_ref[...], q_weight_ref[:, lanes], preferred_element_type=f32)
        inner = inner + q_bias_ref[:, lanes]
        gate = sigmoid(inner)
        smooth = inner * gate
        slope_ref[:, lanes] = (gate + smooth * (1.0 - gate)).astype(bf16)
        total_term = pooled[:, lanes]
        for at in range(PER):
            total_term = total_term + share[at] * smooth[at * targets : (at + 1) * targets]
        pooled[:, lanes] = total_term

    @pl.when(step == pl.num_programs(0) - 1)
    def _():
        w_copy.wait()
        width = own_ref.shape[1]
        hidden = active_ref.shape[1]
        joined = jnp.concatenate([own_ref[...], pooled[...].astype(bf16)], axis=1)
        outer = jnp.concatenate(
            [
                jnp.dot(joined, columns(w_ref, part, 0, width + hidden), preferred_element_type=f32)
                for part in range(w_ref.shape[0] // 2)
            ],
            axis=1,
        )
        outer = outer + w_bias_ref[...]
        gate = sigmoid(outer)
        active = outer * gate
        active_ref[...] = active
        outer_slope_ref[...] = gate + active * (1.0 - gate)
        scaling = lax.rsqrt(jnp.mean(active * active, axis=1, keepdims=True) + epsilon)
        embedded = (active * scaling).astype(bf16)
        embedded_ref[...] = embedded
        queries = embedded[:PAIRS].astype(f32)
        close = jnp.sum(queries * embedded[PAIRS : 2 * PAIRS].astype(f32), axis=1, keepdims=True)
        close = close / hidden
        first = close.astype(bf16).astype(f32)
        second = (close - first).astype(bf16).astype(f32)
        third = close - first - second
        lanes = lax.broadcasted_iota(jnp.int32, (PAIRS, EXTRA), 1)
        pieces = jnp.where(
            lanes == 0, first, jnp.where(lanes == 1, second, jnp.where(lanes == 2, third, 0.0))
        )
        payload_ref[:PAIRS, :hidden] = embedded[:PAIRS]
        payload_ref[PAIRS:, :hidden] = embedded[2 * PAIRS :]
        payload_ref[:PAIRS, hidden:] = pieces.astype(bf16)
        payload_ref[PAIRS:, hidden:] = jnp.zeros((NEG_DEV, EXTRA), bf16)


def whole(shape):
    return pl.BlockSpec(shape, lambda step: (0,) * len(shape))


def forward(fetched, importance, q_weight, q_bias, w_full, w_bias):
    targets = importance.shape[0]
    width, hidden = q_weight.shape
    sent = PAIRS + NEG_DEV
    return pl.pallas_call(
        forward_kernel,
        grid=(K // PER,),
        in_specs=[
            pl.BlockSpec((targets, width), lambda step: (K, 0)),
            pl.BlockSpec((targets * PER, width), lambda step: (step, 0)),
            whole(importance.shape),
            whole(q_weight.shape),
            whole((1, hidden)),
            pl.BlockSpec(memory_space=pl.ANY),
            whole((1, hidden)),
        ],
        out_specs=[
            pl.BlockSpec((targets * PER, hidden), lambda step: (step, 0)),
            whole((targets, hidden)),
            whole((targets, hidden)),
            whole((targets, hidden)),
            whole((sent, hidden + EXTRA)),
        ],
        out_shape=(
            jax.ShapeDtypeStruct((targets * K, hidden), bf16),
            jax.ShapeDtypeStruct((targets, hidden), bf16),
            jax.ShapeDtypeStruct((targets, hidden), f32),
            jax.ShapeDtypeStruct((targets, hidden), f32),
            jax.ShapeDtypeStruct((sent, hidden + EXTRA), bf16),
        ),
        scratch_shapes=[
            pltpu.VMEM((targets, hidden), f32),
            pltpu.VMEM(w_full.shape, bf16),
            pltpu.SemaphoreType.DMA,
        ],
        compiler_params=params(),
        name="forward",
    )(fetched, fetched, importance, q_weight, q_bias[None, :], w_full, w_bias[None, :])


def backward_kernel(
    fetched_ref,
    importance_ref,
    w_far_ref,
    slope_far_ref,
    embedded_ref,
    active_ref,
    outer_slope_ref,
    group_ref,
    grad_ref,
    d_inner,
    w_ref,
    w_arrived,
    slope_ref,
    slope_arrived,
):
    w_copy = pltpu.make_async_copy(w_far_ref, w_ref, w_arrived)
    slope_copy = pltpu.make_async_copy(slope_far_ref, slope_ref, slope_arrived)
    w_copy.start()
    slope_copy.start()
    targets, hidden = active_ref.shape
    members = group_ref.shape[0]
    negatives_count = members * NEG_DEV

    embedded = embedded_ref[...]
    queries = embedded[:PAIRS]
    positives = embedded[PAIRS : 2 * PAIRS].astype(f32)
    negatives = embedded[2 * PAIRS :]
    group_queries = group_ref[:, :PAIRS, :hidden].reshape(members * PAIRS, hidden)
    group_negatives = group_ref[:, PAIRS:, :hidden].reshape(negatives_count, hidden)
    pieces = group_ref[:, :PAIRS, hidden:].reshape(members * PAIRS, EXTRA).astype(f32)
    group_close = jnp.sum(pieces, axis=1, keepdims=True)
    coef_factor = score_scale / (negatives_count * hidden)
    wide_queries = queries.astype(f32)
    close = jnp.sum(wide_queries * positives, axis=1, keepdims=True) / hidden
    far = row_dot(queries, group_negatives) / hidden
    margins = score_scale * (far - close) + margin
    coef = (sigmoid(margins) * coef_factor).astype(bf16)
    toward = jnp.dot(coef, group_negatives, preferred_element_type=f32)
    row_total = jnp.sum(coef.astype(f32), axis=1, keepdims=True)
    softplus = jnp.maximum(margins, 0.0) + jnp.log1p(jnp.exp(-jnp.abs(margins)))
    objective = jnp.sum(jnp.sum(softplus, axis=1, keepdims=True), axis=0, keepdims=True)
    objective = objective / negatives_count
    group_far = row_dot(group_queries, negatives) / hidden
    group_margins = score_scale * (group_far - group_close) + margin
    group_coef = (sigmoid(group_margins) * coef_factor).astype(bf16)
    d_embed = jnp.concatenate(
        [
            toward - row_total * positives,
            -row_total * wide_queries,
            col_dot(group_coef, group_queries),
        ],
        axis=0,
    )
    active = active_ref[...]
    scaling = lax.rsqrt(jnp.mean(active * active, axis=1, keepdims=True) + epsilon)
    along = jnp.sum(d_embed * active, axis=1, keepdims=True)
    d_active = scaling * (d_embed - active * (along * scaling * scaling / hidden))
    d_outer = (d_active * outer_slope_ref[...]).astype(bf16)
    w_copy.wait()
    width = fetched_ref.shape[1]
    pair = 2 * w_ref.shape[2]
    sums = jnp.zeros((targets, hidden), f32)
    for part in range(w_ref.shape[0] // 2):
        lanes = slice(part * pair, (part + 1) * pair)
        sums = sums + row_dot(d_outer[:, lanes], columns(w_ref, part, width, width + hidden))
    d_pooled = sums

    shares = shares_of(importance_ref[...])
    sums = jnp.zeros((1, hidden), f32)
    slope_copy.wait()
    for at in range(K):
        rows = slice(at * targets, (at + 1) * targets)
        d_near = (column(shares, at) * d_pooled * slope_ref[rows, :].astype(f32)).astype(bf16)
        d_inner[rows, :] = d_near
        sums = sums + jnp.sum(d_near.astype(f32), axis=0, keepdims=True)

    near = fetched_ref[: K * targets, :]
    grad_ref[:, :hidden] = col_dot(near, d_inner[...]).astype(bf16)
    grad_ref[:, hidden:] = jnp.zeros((grad_ref.shape[0], EXTRA), bf16)
    rows = lax.broadcasted_iota(jnp.int32, (16, EXTRA), 0)
    small = jnp.zeros((16, EXTRA), f32)
    for part in range(hidden // EXTRA):
        piece = sums[:, part * EXTRA : (part + 1) * EXTRA]
        small = jnp.where(rows == part, piece, small)
    first = objective.astype(bf16).astype(f32)
    small = jnp.where(rows == hidden // EXTRA, first, small)
    small = jnp.where(rows == hidden // EXTRA + 1, objective - first, small)
    grad_ref[:16, hidden:] = small.astype(bf16)


def backward(fetched, importance, w_full, slope, embedded, active, outer_slope, group):
    targets, hidden = active.shape
    width = fetched.shape[1]
    far = pl.BlockSpec(memory_space=pl.ANY)
    near = pl.BlockSpec(memory_space=pltpu.VMEM)
    return pl.pallas_call(
        backward_kernel,
        in_specs=[near, near, far, far, near, near, near, near],
        out_specs=near,
        out_shape=jax.ShapeDtypeStruct((width, hidden + EXTRA), bf16),
        scratch_shapes=[
            pltpu.VMEM((targets * K, hidden), bf16),
            pltpu.VMEM(w_full.shape, bf16),
            pltpu.SemaphoreType.DMA,
            pltpu.VMEM(slope.shape, bf16),
            pltpu.SemaphoreType.DMA,
        ],
        compiler_params=params(36),
        name="backward",
    )(fetched, importance, w_full, slope, embedded, active, outer_slope, group)


def exchange(values, axes):
    return lax.all_to_all(values, axes, split_axis=0, concat_axis=0, tiled=True)


def spread(values, axes):
    count = lax.axis_size(axes)
    return exchange(jnp.broadcast_to(values[None], (count,) + values.shape), axes)


def total(values, axes):
    count = lax.axis_size(axes)
    share = values.shape[0] // count
    parts = exchange(values.reshape((count, share) + values.shape[1:]), axes)
    return jnp.sum(parts.astype(f32), axis=0)


def body(slab, scales, owner, local, importance, q_weight, q_bias, w_weight, w_bias):
    pin_count = lax.axis_size(PIN)
    targets = importance.shape[0]
    width, hidden = q_weight.shape
    lanes = hidden // lax.axis_size(GRP)
    rows = w_weight.shape[0]
    w_part = lax.dynamic_slice_in_dim(w_weight, lax.axis_index(GRP) * lanes, lanes, 1)
    sent, ready, target, slot = plan(slab, scales, w_part, owner, local, pin_count)
    sent = exchange(sent.reshape(pin_count, PIECE, width + lanes), PIN)
    table = sent[:, :, :width].reshape(pin_count * PIECE, width)
    table = jnp.concatenate([ready, table], axis=0)
    digits = sent[:, COPIED + 2, :256]
    ids = digits.astype(jnp.int32)
    asked = ids[:, :ALL_SLOTS] * DIGIT + ids[:, 128 : 128 + ALL_SLOTS]
    picked = jnp.take(table, asked[:, :SLOTS].reshape(-1), axis=0, mode="clip")
    got = exchange(picked.reshape(pin_count, SLOTS, width), PIN).reshape(-1, width)
    w_part = sent[:, COPIED : COPIED + 2, :width].reshape(pin_count, rows - PIECE, lanes)
    w_part = jnp.concatenate([sent[:, :, width:], w_part], axis=1)
    w_part = w_part.reshape(pin_count * rows, lanes)
    over = jnp.max(sent[:, COPIED + 2, 127])
    w_part = jnp.concatenate([w_part, jnp.broadcast_to(over, (16, lanes))], axis=0)
    w_full = lax.all_gather(w_part, GRP, axis=0, tiled=False)
    over = jnp.max(w_full[:, -1, :1].astype(f32)) > 0.5

    def ordered(values):
        return jnp.roll(values.reshape(targets, K + 1).T, -1, axis=0).reshape(-1)

    target, slot = ordered(target), ordered(slot)
    late = slot >= SLOTS
    fetched = jnp.take(got, jnp.where(late, 0, target * SLOTS + slot), axis=0, mode="clip")

    def second_exchange(fetched):
        more = ALL_SLOTS - SLOTS
        picked = jnp.take(table, asked[:, SLOTS:].reshape(-1), axis=0, mode="clip")
        got = exchange(picked.reshape(pin_count, more, width), PIN).reshape(-1, width)
        place = jnp.where(late, target * more + slot - SLOTS, 0)
        return jnp.where(late[:, None], jnp.take(got, place, axis=0, mode="clip"), fetched)

    fetched = lax.cond(over, second_exchange, lambda fetched: fetched, fetched)
    slope, embedded, active, outer_slope, payload = forward(
        fetched, importance, q_weight, q_bias, w_full, w_bias
    )
    group = spread(spread(payload, "x"), "core")
    group = group.reshape((-1,) + payload.shape)
    grads = backward(fetched, importance, w_full, slope, embedded, active, outer_slope, group)
    grads = total(grads, "core").astype(bf16)
    grads = total(grads, PIN)
    grads = jnp.sum(spread(grads, "x"), axis=0)
    loss_row = hidden // EXTRA
    grads = spread(grads.astype(bf16), PIN).reshape(-1, hidden + EXTRA)
    grads = spread(grads, "core").reshape(-1, hidden + EXTRA)
    grad_q = grads[:, :hidden].astype(f32)
    grad_bias = grads[:loss_row, hidden:].astype(f32).reshape(-1)
    objective = jnp.sum(grads[loss_row : loss_row + 2, hidden].astype(f32))
    devices = pin_count * lax.axis_size(GRP)
    loss = objective / (PAIRS * devices)
    return (embedded, grad_q, grad_bias, loss)


def solution(mesh):
    devices = mesh.devices.reshape(8, 8, 4, 2)
    fine = Mesh(devices, PIN + GRP)
    in_specs = (
        P(PIN, None),
        P(PIN, None),
        P(PIN + GRP, None),
        P(PIN + GRP, None),
        P(PIN + GRP, None),
        P(),
        P(),
        P(PIN, None),
        P(),
    )
    out_specs = (P(PIN + GRP, None), P(), P(), P())
    return jax.shard_map(body, mesh=fine, in_specs=in_specs, out_specs=out_specs, check_vma=False)
```

```python
import jax
import jax.numpy as jnp
from jax import lax
from jax.experimental import pallas as pl
from jax.experimental.pallas import tpu as pltpu
from jax.sharding import Mesh
from jax.sharding import PartitionSpec as P

K = 10
PAIRS = 64
NEG_DEV = 64
SLOTS = 40
ALL_SLOTS = 80
PIECE = 16
COPIED = 13
TARGETS = (44, 36, 38, 39, 40)
DIGIT = 32
PER = 5
CHUNK = 256
EXTRA = 128

margin = 0.5
score_scale = 8.0
epsilon = 1e-05

PIN = ("y", "z")
GRP = ("x", "core")
bf16 = jnp.bfloat16
f32 = jnp.float32


def sigmoid(value):
    return 0.5 * jnp.tanh(0.5 * value) + 0.5


def params(megabytes=24):
    return pltpu.CompilerParams(vmem_limit_bytes=megabytes * 1024 * 1024)


def row_dot(a, b):
    return lax.dot_general(a, b, (((1,), (1,)), ((), ())), preferred_element_type=f32)


def col_dot(a, b):
    return lax.dot_general(a, b, (((0,), (0,)), ((), ())), preferred_element_type=f32)


def before(parts):
    width = parts[0].shape[1]
    earlier = lax.broadcasted_iota(jnp.int32, (width, width), 0) < lax.broadcasted_iota(
        jnp.int32, (width, width), 1
    )
    inside = jnp.dot(
        jnp.concatenate([part.astype(bf16) for part in parts], axis=0),
        earlier.astype(f32).astype(bf16),
        preferred_element_type=f32,
    )
    high = parts[0].shape[0]
    sums, count = [], jnp.zeros((high, 1), f32)
    for block, part in enumerate(parts):
        sums.append(inside[block * high : (block + 1) * high] + count)
        count = count + jnp.sum(part, axis=1, keepdims=True)
    return sums


def pick(wide, values):
    return jnp.sum(wide * values, axis=0, keepdims=True)


def plan_kernel(
    row_ref,
    slab_far_ref,
    scales_ref,
    w_ref,
    sent_ref,
    ready_ref,
    target_ref,
    slot_ref,
    slab_ref,
    slab_arrived,
):
    slab_copy = pltpu.make_async_copy(slab_far_ref, slab_ref, slab_arrived)
    slab_copy.start()
    blocks, width = row_ref.shape
    pins = ready_ref.shape[0]
    owners = pins // PIECE
    ids = lax.broadcasted_iota(jnp.int32, (owners, width), 0)
    own = [row_ref[block : block + 1, :] // pins for block in range(blocks)]
    local = [row_ref[block : block + 1, :] % pins for block in range(blocks)]
    first = [(one == ids).astype(f32) for one in own]
    second = [((one // PIECE) == ids).astype(f32) for one in local]
    free = [jnp.where(one % PIECE < COPIED, 1.0, 0.0) for one in local]
    moved = [jnp.zeros((1, width), f32)] * blocks
    load = sum(jnp.sum(wide, axis=1, keepdims=True) for wide in first)
    for goal in TARGETS:
        excess = jnp.maximum(load - goal, 0.0)
        spare = jnp.maximum(goal - load, 0.0)
        over = [pick(wide, excess) for wide in first]
        room = [pick(wide, spare) for wide in second]
        movable = [
            jnp.where((most > 0.0) & (least > 0.0), one, 0.0)
            for most, least, one in zip(over, room, free)
        ]
        queue = before([wide * one for wide, one in zip(second, movable)])
        kept = [
            jnp.where(pick(wide, sums) < least, one, 0.0)
            for wide, sums, least, one in zip(second, queue, room, movable)
        ]
        gone = before([wide * one for wide, one in zip(first, kept)])
        new = [
            jnp.where(pick(wide, sums) < most, one, 0.0)
            for wide, sums, most, one in zip(first, gone, over, kept)
        ]
        moved = [one + more for one, more in zip(moved, new)]
        free = [one - more for one, more in zip(free, new)]
        change = sum((there - here) * more for here, there, more in zip(first, second, new))
        load = load + jnp.sum(change, axis=1, keepdims=True)
    holder = [here + (there - here) * one for here, there, one in zip(first, second, moved)]
    rank = before(holder)
    slot_ids = lax.broadcasted_iota(jnp.int32, (width, width), 0)
    high_sum = jnp.zeros((owners, width), f32)
    low_sum = jnp.zeros((owners, width), f32)
    widest = jnp.zeros((1, width), jnp.int32)
    for block in range(blocks):
        slot = pick(holder[block], rank[block]).astype(jnp.int32)
        other = moved[block] > 0.0
        row = jnp.where(
            other,
            owners * PIECE + own[block] * PIECE + local[block] % PIECE,
            local[block],
        )
        wide = holder[block].astype(bf16)
        there = (slot == slot_ids).astype(f32)
        high_sum = high_sum + row_dot(wide, (there * (row // DIGIT).astype(f32)).astype(bf16))
        low_sum = low_sum + row_dot(wide, (there * (row % DIGIT).astype(f32)).astype(bf16))
        widest = jnp.maximum(widest, slot)
        target_ref[block : block + 1, :] = jnp.where(other, local[block] // PIECE, own[block])
        slot_ref[block : block + 1, :] = slot
    late = (jnp.max(widest, axis=1, keepdims=True) >= SLOTS).astype(f32)
    last = lax.broadcasted_iota(jnp.int32, (owners, width), 1) == width - 1
    digits = jnp.concatenate([jnp.where(last, late, high_sum), low_sum], axis=1).astype(bf16)
    slab_copy.wait()
    block = slab_ref.shape[1] // scales_ref.shape[1]
    for part in range(scales_ref.shape[1]):
        lanes = slice(part * block, (part + 1) * block)
        scale = scales_ref[:, part : part + 1].astype(f32)
        ready_ref[:, lanes] = (slab_ref[:, lanes].astype(f32) * scale).astype(bf16)
    here = COPIED + 2
    piece_row = lax.broadcasted_iota(jnp.int32, (pins, owners), 1) * PIECE + here
    rows = lax.broadcasted_iota(jnp.int32, (pins, owners), 0)
    digits = jnp.dot(
        (rows == piece_row).astype(f32).astype(bf16), digits, preferred_element_type=f32
    )
    place = lax.broadcasted_iota(jnp.int32, (pins, block), 0) % PIECE
    w_part = w_ref[...].astype(f32)
    for part in range(scales_ref.shape[1]):
        lanes = slice(part * block, (part + 1) * block)
        values = ready_ref[:, lanes].astype(f32)
        values = jnp.where(place == COPIED, w_part[PIECE + part : PIECE + part + 1], values)
        values = jnp.where(place == COPIED + 1, w_part[PIECE + 4 + part : PIECE + 5 + part], values)
        if part < 2:
            values = jnp.where(place == here, digits[:, lanes], values)
        sent_ref[:, lanes] = values.astype(bf16)
    side = jnp.broadcast_to(w_part[None, :PIECE], (owners, PIECE, block)).reshape(pins, block)
    sent_ref[:, scales_ref.shape[1] * block :] = side.astype(bf16)


def plan(slab, scales, w_part, owner, local, owners):
    rows = owner.shape[0]
    pins = slab.shape[0]
    blocks = -(-rows // 128)
    spare = blocks * 128 - rows
    row = (owner * pins + local)[:, 0]
    row = jnp.pad(row, (0, spare), constant_values=owners * pins).reshape(blocks, 128)
    near = pl.BlockSpec(memory_space=pltpu.VMEM)
    sent, ready, target, slot = pl.pallas_call(
        plan_kernel,
        in_specs=[near, pl.BlockSpec(memory_space=pl.ANY), near, near],
        out_shape=(
            jax.ShapeDtypeStruct((pins, slab.shape[1] + w_part.shape[1]), bf16),
            jax.ShapeDtypeStruct(slab.shape, bf16),
            jax.ShapeDtypeStruct((blocks, 128), jnp.int32),
            jax.ShapeDtypeStruct((blocks, 128), jnp.int32),
        ),
        scratch_shapes=[pltpu.VMEM(slab.shape, bf16), pltpu.SemaphoreType.DMA],
        compiler_params=params(),
        name="plan",
    )(row, slab, scales, w_part)
    return sent, ready, target.reshape(-1)[:rows], slot.reshape(-1)[:rows]


def shares_of(importance):
    return importance / jnp.sum(importance, axis=1, keepdims=True)


def column(values, at):
    lanes = lax.broadcasted_iota(jnp.int32, values.shape, 1)
    return jnp.sum(jnp.where(lanes == at, values, 0.0), axis=1, keepdims=True)


def columns(w_ref, part, start, end):
    return jnp.concatenate(
        [w_ref[2 * part, start:end, :], w_ref[2 * part + 1, start:end, :]], axis=1
    )


def forward_kernel(
    own_ref,
    near_ref,
    importance_ref,
    q_weight_ref,
    q_bias_ref,
    w_far_ref,
    w_bias_ref,
    slope_ref,
    embedded_ref,
    active_ref,
    outer_slope_ref,
    payload_ref,
    pooled,
    w_ref,
    w_arrived,
):
    step = pl.program_id(0)
    w_copy = pltpu.make_async_copy(w_far_ref, w_ref, w_arrived)

    @pl.when(step == 0)
    def _():
        w_copy.start()

    targets = pooled.shape[0]
    shares = shares_of(importance_ref[...])
    share = [column(shares, step * PER + at) for at in range(PER)]

    @pl.when(step == 0)
    def _():
        pooled[...] = jnp.zeros_like(pooled)

    for part in range(pooled.shape[1] // CHUNK):
        lanes = slice(part * CHUNK, (part + 1) * CHUNK)
        inner = jnp.dot(near_ref[...], q_weight_ref[:, lanes], preferred_element_type=f32)
        inner = inner + q_bias_ref[:, lanes]
        gate = sigmoid(inner)
        smooth = inner * gate
        slope_ref[:, lanes] = (gate + smooth * (1.0 - gate)).astype(bf16)
        total_term = pooled[:, lanes]
        for at in range(PER):
            total_term = total_term + share[at] * smooth[at * targets : (at + 1) * targets]
        pooled[:, lanes] = total_term

    @pl.when(step == pl.num_programs(0) - 1)
    def _():
        w_copy.wait()
        width = own_ref.shape[1]
        hidden = active_ref.shape[1]
        joined = jnp.concatenate([own_ref[...], pooled[...].astype(bf16)], axis=1)
        outer = jnp.concatenate(
            [
                jnp.dot(joined, columns(w_ref, part, 0, width + hidden), preferred_element_type=f32)
                for part in range(w_ref.shape[0] // 2)
            ],
            axis=1,
        )
        outer = outer + w_bias_ref[...]
        gate = sigmoid(outer)
        active = outer * gate
        active_ref[...] = active
        outer_slope_ref[...] = gate + active * (1.0 - gate)
        scaling = lax.rsqrt(jnp.mean(active * active, axis=1, keepdims=True) + epsilon)
        embedded = (active * scaling).astype(bf16)
        embedded_ref[...] = embedded
        queries = embedded[:PAIRS].astype(f32)
        close = jnp.sum(queries * embedded[PAIRS : 2 * PAIRS].astype(f32), axis=1, keepdims=True)
        close = close / hidden
        first = close.astype(bf16).astype(f32)
        second = (close - first).astype(bf16).astype(f32)
        third = close - first - second
        lanes = lax.broadcasted_iota(jnp.int32, (PAIRS, EXTRA), 1)
        pieces = jnp.where(
            lanes == 0, first, jnp.where(lanes == 1, second, jnp.where(lanes == 2, third, 0.0))
        )
        payload_ref[:PAIRS, :hidden] = embedded[:PAIRS]
        payload_ref[PAIRS:, :hidden] = embedded[2 * PAIRS :]
        payload_ref[:PAIRS, hidden:] = pieces.astype(bf16)
        payload_ref[PAIRS:, hidden:] = jnp.zeros((NEG_DEV, EXTRA), bf16)


def whole(shape):
    return pl.BlockSpec(shape, lambda step: (0,) * len(shape))


def forward(fetched, importance, q_weight, q_bias, w_full, w_bias):
    targets = importance.shape[0]
    width, hidden = q_weight.shape
    sent = PAIRS + NEG_DEV
    return pl.pallas_call(
        forward_kernel,
        grid=(K // PER,),
        in_specs=[
            pl.BlockSpec((targets, width), lambda step: (K, 0)),
            pl.BlockSpec((targets * PER, width), lambda step: (step, 0)),
            whole(importance.shape),
            whole(q_weight.shape),
            whole((1, hidden)),
            pl.BlockSpec(memory_space=pl.ANY),
            whole((1, hidden)),
        ],
        out_specs=[
            pl.BlockSpec((targets * PER, hidden), lambda step: (step, 0)),
            whole((targets, hidden)),
            whole((targets, hidden)),
            whole((targets, hidden)),
            whole((sent, hidden + EXTRA)),
        ],
        out_shape=(
            jax.ShapeDtypeStruct((targets * K, hidden), bf16),
            jax.ShapeDtypeStruct((targets, hidden), bf16),
            jax.ShapeDtypeStruct((targets, hidden), f32),
            jax.ShapeDtypeStruct((targets, hidden), f32),
            jax.ShapeDtypeStruct((sent, hidden + EXTRA), bf16),
        ),
        scratch_shapes=[
            pltpu.VMEM((targets, hidden), f32),
            pltpu.VMEM(w_full.shape, bf16),
            pltpu.SemaphoreType.DMA,
        ],
        compiler_params=params(),
        name="forward",
    )(fetched, fetched, importance, q_weight, q_bias[None, :], w_full, w_bias[None, :])


def backward_kernel(
    fetched_ref,
    importance_ref,
    w_far_ref,
    slope_far_ref,
    embedded_ref,
    active_ref,
    outer_slope_ref,
    group_ref,
    grad_ref,
    d_inner,
    w_ref,
    w_arrived,
    slope_ref,
    slope_arrived,
):
    w_copy = pltpu.make_async_copy(w_far_ref, w_ref, w_arrived)
    slope_copy = pltpu.make_async_copy(slope_far_ref, slope_ref, slope_arrived)
    w_copy.start()
    slope_copy.start()
    targets, hidden = active_ref.shape
    members = group_ref.shape[0]
    negatives_count = members * NEG_DEV

    embedded = embedded_ref[...]
    queries = embedded[:PAIRS]
    positives = embedded[PAIRS : 2 * PAIRS].astype(f32)
    negatives = embedded[2 * PAIRS :]
    group_queries = group_ref[:, :PAIRS, :hidden].reshape(members * PAIRS, hidden)
    group_negatives = group_ref[:, PAIRS:, :hidden].reshape(negatives_count, hidden)
    pieces = group_ref[:, :PAIRS, hidden:].reshape(members * PAIRS, EXTRA).astype(f32)
    group_close = jnp.sum(pieces, axis=1, keepdims=True)
    coef_factor = score_scale / (negatives_count * hidden)
    wide_queries = queries.astype(f32)
    close = jnp.sum(wide_queries * positives, axis=1, keepdims=True) / hidden
    far = row_dot(queries, group_negatives) / hidden
    margins = score_scale * (far - close) + margin
    coef = (sigmoid(margins) * coef_factor).astype(bf16)
    toward = jnp.dot(coef, group_negatives, preferred_element_type=f32)
    row_total = jnp.sum(coef.astype(f32), axis=1, keepdims=True)
    softplus = jnp.maximum(margins, 0.0) + jnp.log1p(jnp.exp(-jnp.abs(margins)))
    objective = jnp.sum(jnp.sum(softplus, axis=1, keepdims=True), axis=0, keepdims=True)
    objective = objective / negatives_count
    group_far = row_dot(group_queries, negatives) / hidden
    group_margins = score_scale * (group_far - group_close) + margin
    group_coef = (sigmoid(group_margins) * coef_factor).astype(bf16)
    d_embed = jnp.concatenate(
        [
            toward - row_total * positives,
            -row_total * wide_queries,
            col_dot(group_coef, group_queries),
        ],
        axis=0,
    )
    active = active_ref[...]
    scaling = lax.rsqrt(jnp.mean(active * active, axis=1, keepdims=True) + epsilon)
    along = jnp.sum(d_embed * active, axis=1, keepdims=True)
    d_active = scaling * (d_embed - active * (along * scaling * scaling / hidden))
    d_outer = (d_active * outer_slope_ref[...]).astype(bf16)
    w_copy.wait()
    width = fetched_ref.shape[1]
    pair = 2 * w_ref.shape[2]
    sums = jnp.zeros((targets, hidden), f32)
    for part in range(w_ref.shape[0] // 2):
        lanes = slice(part * pair, (part + 1) * pair)
        sums = sums + row_dot(d_outer[:, lanes], columns(w_ref, part, width, width + hidden))
    d_pooled = sums

    shares = shares_of(importance_ref[...])
    sums = jnp.zeros((1, hidden), f32)
    slope_copy.wait()
    for at in range(K):
        rows = slice(at * targets, (at + 1) * targets)
        d_near = (column(shares, at) * d_pooled * slope_ref[rows, :].astype(f32)).astype(bf16)
        d_inner[rows, :] = d_near
        sums = sums + jnp.sum(d_near.astype(f32), axis=0, keepdims=True)

    near = fetched_ref[: K * targets, :]
    grad_ref[:, :hidden] = col_dot(near, d_inner[...]).astype(bf16)
    grad_ref[:, hidden:] = jnp.zeros((grad_ref.shape[0], EXTRA), bf16)
    rows = lax.broadcasted_iota(jnp.int32, (16, EXTRA), 0)
    small = jnp.zeros((16, EXTRA), f32)
    for part in range(hidden // EXTRA):
        piece = sums[:, part * EXTRA : (part + 1) * EXTRA]
        small = jnp.where(rows == part, piece, small)
    first = objective.astype(bf16).astype(f32)
    small = jnp.where(rows == hidden // EXTRA, first, small)
    small = jnp.where(rows == hidden // EXTRA + 1, objective - first, small)
    grad_ref[:16, hidden:] = small.astype(bf16)


def backward(fetched, importance, w_full, slope, embedded, active, outer_slope, group):
    targets, hidden = active.shape
    width = fetched.shape[1]
    far = pl.BlockSpec(memory_space=pl.ANY)
    near = pl.BlockSpec(memory_space=pltpu.VMEM)
    return pl.pallas_call(
        backward_kernel,
        in_specs=[near, near, far, far, near, near, near, near],
        out_specs=near,
        out_shape=jax.ShapeDtypeStruct((width, hidden + EXTRA), bf16),
        scratch_shapes=[
            pltpu.VMEM((targets * K, hidden), bf16),
            pltpu.VMEM(w_full.shape, bf16),
            pltpu.SemaphoreType.DMA,
            pltpu.VMEM(slope.shape, bf16),
            pltpu.SemaphoreType.DMA,
        ],
        compiler_params=params(36),
        name="backward",
    )(fetched, importance, w_full, slope, embedded, active, outer_slope, group)


def exchange(values, axes):
    return lax.all_to_all(values, axes, split_axis=0, concat_axis=0, tiled=True)


def spread(values, axes):
    count = lax.axis_size(axes)
    return exchange(jnp.broadcast_to(values[None], (count,) + values.shape), axes)


def total(values, axes):
    count = lax.axis_size(axes)
    share = values.shape[0] // count
    parts = exchange(values.reshape((count, share) + values.shape[1:]), axes)
    return jnp.sum(parts.astype(f32), axis=0)


def body(slab, scales, owner, local, importance, q_weight, q_bias, w_weight, w_bias):
    pin_count = lax.axis_size(PIN)
    targets = importance.shape[0]
    width, hidden = q_weight.shape
    lanes = hidden // lax.axis_size(GRP)
    rows = w_weight.shape[0]
    w_part = lax.dynamic_slice_in_dim(w_weight, lax.axis_index(GRP) * lanes, lanes, 1)
    sent, ready, target, slot = plan(slab, scales, w_part, owner, local, pin_count)
    sent = exchange(sent.reshape(pin_count, PIECE, width + lanes), PIN)
    table = sent[:, :, :width].reshape(pin_count * PIECE, width)
    table = jnp.concatenate([ready, table], axis=0)
    digits = sent[:, COPIED + 2, :256]
    ids = digits.astype(jnp.int32)
    asked = ids[:, :ALL_SLOTS] * DIGIT + ids[:, 128 : 128 + ALL_SLOTS]
    picked = jnp.take(table, asked[:, :SLOTS].reshape(-1), axis=0, mode="clip")
    got = exchange(picked.reshape(pin_count, SLOTS, width), PIN).reshape(-1, width)
    w_part = sent[:, COPIED : COPIED + 2, :width].reshape(pin_count, rows - PIECE, lanes)
    w_part = jnp.concatenate([sent[:, :, width:], w_part], axis=1)
    w_part = w_part.reshape(pin_count * rows, lanes)
    over = jnp.max(sent[:, COPIED + 2, 127])
    w_part = jnp.concatenate([w_part, jnp.broadcast_to(over, (16, lanes))], axis=0)
    w_full = lax.all_gather(w_part, GRP, axis=0, tiled=False)
    over = jnp.max(w_full[:, -1, :1].astype(f32)) > 0.5

    def ordered(values):
        return jnp.roll(values.reshape(targets, K + 1).T, -1, axis=0).reshape(-1)

    target, slot = ordered(target), ordered(slot)
    late = over & (slot >= SLOTS)
    fetched = jnp.take(got, jnp.where(late, 0, target * SLOTS + slot), axis=0, mode="clip")

    def second_exchange(fetched):
        more = ALL_SLOTS - SLOTS
        picked = jnp.take(table, asked[:, SLOTS:].reshape(-1), axis=0, mode="clip")
        got = exchange(picked.reshape(pin_count, more, width), PIN).reshape(-1, width)
        place = jnp.where(late, target * more + slot - SLOTS, 0)
        return jnp.where(late[:, None], jnp.take(got, place, axis=0, mode="clip"), fetched)

    fetched = lax.cond(over, second_exchange, lambda fetched: fetched, fetched)
    slope, embedded, active, outer_slope, payload = forward(
        fetched, importance, q_weight, q_bias, w_full, w_bias
    )
    group = spread(spread(payload, "x"), "core")
    group = group.reshape((-1,) + payload.shape)
    grads = backward(fetched, importance, w_full, slope, embedded, active, outer_slope, group)
    grads = total(grads, "core").astype(bf16)
    grads = total(grads, PIN)
    grads = jnp.sum(spread(grads, "x"), axis=0)
    loss_row = hidden // EXTRA
    grads = spread(grads.astype(bf16), PIN).reshape(-1, hidden + EXTRA)
    grads = spread(grads, "core").reshape(-1, hidden + EXTRA)
    grad_q = grads[:, :hidden].astype(f32)
    grad_bias = grads[:loss_row, hidden:].astype(f32).reshape(-1)
    objective = jnp.sum(grads[loss_row : loss_row + 2, hidden].astype(f32))
    devices = pin_count * lax.axis_size(GRP)
    loss = objective / (PAIRS * devices)
    return (embedded, grad_q, grad_bias, loss)


def solution(mesh):
    devices = mesh.devices.reshape(8, 8, 4, 2)
    fine = Mesh(devices, PIN + GRP)
    in_specs = (
        P(PIN, None),
        P(PIN, None),
        P(PIN + GRP, None),
        P(PIN + GRP, None),
        P(PIN + GRP, None),
        P(),
        P(),
        P(PIN, None),
        P(),
    )
    out_specs = (P(PIN + GRP, None), P(), P(), P())
    return jax.shard_map(body, mesh=fine, in_specs=in_specs, out_specs=out_specs, check_vma=False)
```
